256 devices in a mesh: blk: 32 (over y, z), head: 2 (over core), clip: 4 (over x).
Axes of the slice: x: 4, y: 4, z: 8, core: 2. Of those that a mesh axis runs over, the one named last changes fastest.
Arguments:
- tokens: bfloat16 [36864, 1536], P(('clip', 'blk', 'head')), parts along dimension 0, may hold values from -6 to 6
- modulation: float32 [12, 1536], P('clip'), parts along dimension 0, may hold values from -3 to 3
- w_qkv: bfloat16 [1536, 3, 1536], P(None, None, 'head'), may hold values from -0.25 to 0.25
- w_out: bfloat16 [1536, 1536], P('head'), may hold values from -0.15625 to 0.15625
- w_cross: bfloat16 [1536, 1536], P(None, 'head'), may hold values from -0.15625 to 0.15625
- q_gain: float32 [128], replicated, may hold values from 0.5 to 6
- k_gain: float32 [128], replicated, may hold values from 0.5 to 6
- cross_gain: float32 [128], replicated, may hold values from 0.5 to 6
- scene_keys: bfloat16 [8192, 1536], P(('clip', 'blk'), 'head'), parts along dimension 0, may hold values from -40 to 40
- scene_values: bfloat16 [8192, 1536], P(('clip', 'blk'), 'head'), parts along dimension 0, may hold values from -6 to 6
Outputs:
- hidden: bfloat16 [36864, 1536], P(('clip', 'blk', 'head')), parts along dimension 0
- cross_context: bfloat16 [36864, 1536], P(('clip', 'blk'), 'head'), parts along dimension 0
The draws below stay inside these ranges and needn't reach their ends.
There are 4 independent parts, one for each index of `clip`. The reference program is written for one: setup_inputs(seed, part) draws one part's arguments, and reference() takes and returns one part's arrays. A program takes and returns all parts, laid end to end along the dimension named above; an argument that names none is the same for every part. Nothing has to cross between parts.
All inputs are finite; a program needn't handle non-finite values.
Results may differ from the reference program's by a relative error of at most 0.015.
The reference program's roundings to bfloat16 on the way (of `modulated`, `context` and `cross_queries`) count: a program that leaves them out, or rounds other values in their place, can miss the bound.
Values may be sent and summed in bfloat16 or wider, within the bound.
A program may use at most 128 MiB of HBM per device.

```python
import jax
import jax.numpy as jnp
from jax import lax

D = 1536
HEADS = 12
HD = 128
S = 9216
SC = 2048


def draw_tokens(key, part):
    base = jax.random.normal(key, (S, D), jnp.float32)
    return jnp.clip(base, -6.0, 6.0).astype(jnp.bfloat16)


def draw_w_qkv(key, part):
    base = jax.random.normal(key, (D, 3, D), jnp.float32) / D ** 0.5
    return jnp.clip(base, -0.25, 0.25).astype(jnp.bfloat16)


def gain_common(key, salt):
    own_key = jax.random.fold_in(key, salt)
    return jnp.exp(jax.random.uniform(own_key, (HD,), jnp.float32, 0.26, 0.83))


def draw_q_gain(key, part):
    return gain_common(key, 1)


def draw_k_gain(key, part):
    return gain_common(key, 2)


def draw_cross_gain(key, part):
    return gain_common(key, 3)


def draw_scene_keys(key, part):
    base = jax.random.normal(key, (SC, D), jnp.float32)
    return jnp.clip(base, -40.0, 40.0).astype(jnp.bfloat16)


def levels(rng, extent, pieces, least, top_value):
    level = 1.0
    for axis_at, shards_of in pieces:
        steps = jax.random.uniform(jax.random.fold_in(jax.random.fold_in(rng, 6), axis_at), (shards_of,), jnp.float32, least / len(pieces), top_value / len(pieces))
        level = level * jnp.repeat(jnp.exp(steps), extent[axis_at] // shards_of).reshape((-1,) + (1,) * (len(extent) - 1 - axis_at))
    return level


def scatter_about(stream_key, dims, scale, bound, cuts=(), held_as=jnp.bfloat16):
    values = jax.random.normal(stream_key, dims, jnp.float32) * scale
    if len(cuts) > 0:
        values = levels(stream_key, dims, cuts, -0.22, 0.18) * values
    return jnp.clip(values, min=-bound, max=bound).astype(held_as)


def setup_inputs(seed: int = 0, part: int = 0) -> dict:
    arg_keys = jax.random.split(jax.random.key(seed), 11)
    own_keys = jax.random.split(jax.random.fold_in(arg_keys[10], part), 11)
    return {
        "tokens": draw_tokens(jax.random.fold_in(jax.random.fold_in(arg_keys[10], part), 71), part),
        "modulation": scatter_about(own_keys[1], (3, D), 0.5, 3.0, (), jnp.float32),
        "w_qkv": draw_w_qkv(jax.random.fold_in(arg_keys[10], 71), part),
        "w_out": scatter_about(arg_keys[3], (D, D), D ** -0.5, 0.15625, ((0, 2),)),
        "w_cross": scatter_about(arg_keys[4], (D, D), D ** -0.5, 0.15625, ((1, 2),)),
        "q_gain": draw_q_gain(jax.random.fold_in(arg_keys[10], 71), part),
        "k_gain": draw_k_gain(jax.random.fold_in(arg_keys[10], 71), part),
        "cross_gain": draw_cross_gain(jax.random.fold_in(arg_keys[10], 71), part),
        "scene_keys": draw_scene_keys(jax.random.fold_in(jax.random.fold_in(arg_keys[10], part), 71), part),
        "scene_values": scatter_about(own_keys[9], (SC, D), 1.0, 6.0, ((0, 32), (1, 2))),
    }


def head_norm(values, gain):
    rms = lax.optimization_barrier(jnp.mean(values * values, axis=-1, keepdims=True))
    return values * lax.rsqrt(rms + 1e-06) * gain

def attention(queries, keys_all, values_all):
    rows = queries.shape[0]
    block = 512 if rows % 512 == 0 else rows
    scale = 1.0 / HD ** 0.5
    keys_f = keys_all.astype(jnp.float32)
    values_f = values_all.astype(jnp.float32)

    def one_block(query_blk):
        scores = jnp.einsum('rhd,nhd->hrn', query_blk.astype(jnp.float32), keys_f) * scale
        probs = jax.nn.softmax(scores, axis=-1)
        return jnp.einsum('hrn,nhd->rhd', probs, values_f)
    blocks = queries.reshape(rows // block, block, HEADS, HD)
    result = lax.map(one_block, blocks)
    return result.reshape(rows, D)

def reference(tokens, modulation, w_qkv, w_out, w_cross, q_gain, k_gain, cross_gain, scene_keys, scene_values):
    xfloat = tokens.astype(jnp.float32)
    mean = lax.optimization_barrier(jnp.mean(xfloat, axis=-1, keepdims=True))
    var = lax.optimization_barrier(jnp.mean((xfloat - mean) ** 2, axis=-1, keepdims=True))
    normed = (xfloat - mean) * lax.rsqrt(var + 1e-06)
    modulated = (normed * (1.0 + modulation[1]) + modulation[0]).astype(jnp.bfloat16)
    projected = jnp.dot(modulated, w_qkv.reshape(D, 3 * D), preferred_element_type=jnp.float32)
    projected = projected.reshape(S, 3, HEADS, HD)
    queries = head_norm(projected[:, 0], q_gain).astype(jnp.bfloat16)
    keys_n = head_norm(projected[:, 1], k_gain).astype(jnp.bfloat16)
    values = projected[:, 2].astype(jnp.bfloat16)
    context = attention(queries, keys_n, values).astype(jnp.bfloat16)
    attn = jnp.dot(context, w_out, preferred_element_type=jnp.float32)
    hidden = (xfloat + modulation[2] * attn).astype(jnp.bfloat16)
    cross_proj = jnp.dot(hidden, w_cross, preferred_element_type=jnp.float32).reshape(S, HEADS, HD)
    cross_queries = head_norm(cross_proj, cross_gain).astype(jnp.bfloat16)
    cross_context = attention(cross_queries, scene_keys.reshape(SC, HEADS, HD), scene_values.reshape(SC, HEADS, HD))
    return (hidden, cross_context.astype(jnp.bfloat16))
```

```python
import functools

import jax
import jax.numpy as jnp
from jax import lax
from jax.experimental import pallas as pl
from jax.experimental.pallas import tpu as pltpu
from jax.sharding import PartitionSpec as P

HD = 128
NY, NZ = 4, 8
F32, BF16 = jnp.float32, jnp.bfloat16
MESH = pl.DeviceIdType.MESH
SCALE2 = 1.4426950408889634 / HD**0.5
SAFE_EXPONENT = 96.0
MAIN = (0, 2, 3, 5)
SHARED = (1, 1, 4, 4)
ORDER = ((0, 4), (1, 7), (2, 6), (3, 5))


def head_norm(values, gain):
    rms = jnp.mean(values * values, axis=-1, keepdims=True)
    return values * lax.rsqrt(rms + 1e-06) * gain


def place():
    blk = lax.axis_index("blk")
    return blk // NZ, lax.rem(blk, NZ), lax.axis_index("head")


def device(y, z, core):
    return {"blk": y * NZ + z, "head": core}


def slot_of(d):
    s = d // 4
    chunk = d * (1 - s) + lax.rem(8 - d, 4) * s
    return 2 * chunk + s


def put(here, src, dst, send_sem, recv_sem, target, same):
    @pl.when(same)
    def _():
        pltpu.make_async_copy(src, dst, recv_sem).start()

    @pl.when(jnp.logical_not(same))
    def _():
        pltpu.make_async_remote_copy(src, dst, send_sem, recv_sem, target, MESH).start()


def sent(src, send_sem, same):
    @pl.when(jnp.logical_not(same))
    def _():
        pltpu.make_async_copy(src, src, send_sem).wait()


def landed(dst, recv_sem):
    pltpu.make_async_copy(dst, dst, recv_sem).wait()


def greet(y, z, core, with_y):
    barrier = pltpu.get_barrier_semaphore()
    for d in range(NZ):
        for e in range(2):
            if d or e:
                to = device(y, lax.rem(z + d, NZ), lax.rem(core + e, 2))
                pl.semaphore_signal(barrier, inc=1, device_id=to, device_id_type=MESH)
    if with_y:
        for d in range(1, NY):
            to = device(lax.rem(y + d, NY), z, core)
            pl.semaphore_signal(barrier, inc=1, device_id=to, device_id_type=MESH)
    pl.semaphore_wait(barrier, 15 + (3 if with_y else 0))


def attend(use_max, q, k, v, acc, best, rows):
    s = lax.dot_general(q, k, (((1,), (1,)), ((), ())), preferred_element_type=F32)
    wide = jnp.concatenate([v, jnp.ones_like(v)], axis=1)
    if use_max:
        s = s * SCALE2
        old = best[rows, :]
        new = jnp.maximum(old, jnp.max(s, axis=1, keepdims=True))
        best[rows, :] = new
        p = jnp.exp2(s - new[:, :1]).astype(BF16)
        factor = jnp.exp2(old - new)
        kept = acc[rows, :] * jnp.concatenate([factor, factor], axis=1)
        acc[rows, :] = kept + jnp.dot(p, wide, preferred_element_type=F32)
    else:
        p = jnp.exp2(s * SCALE2).astype(BF16)
        acc[rows, :] += jnp.dot(p, wide, preferred_element_type=F32)


def send_queries(y, z, core, half, qm_ref, qs_ref, qbuf, s_q, r_q):
    for d in (4, 0, 1, 7, 2, 6, 3, 5):
        to_z = lax.rem(z + NZ - d, NZ)

        @pl.when(to_z // 4 == core)
        def _():
            j = to_z - 4 * core
            for u in range(2):
                to = device(y, to_z, u)
                same = jnp.logical_and(to_z == z, core == u)
                rows = pl.ds(u * half, half)
                put(None, qm_ref.at[j, rows, :], qbuf.at[pl.ds(z * half, half), :],
                    s_q.at[d, u, 0], r_q.at[z], to, same)

                @pl.when(lax.rem(to_z, 2) == lax.rem(z, 2))
                def _():
                    put(None, qs_ref.at[j, rows, :], qbuf.at[pl.ds((NZ + z // 2) * half, half), :],
                        s_q.at[d, u, 1], r_q.at[NZ + z // 2], to, same)


def queries_sent(y, z, core, half, qm_ref, qs_ref, s_q):
    for d in range(NZ):
        to_z = lax.rem(z + NZ - d, NZ)

        @pl.when(to_z // 4 == core)
        def _():
            for u in range(2):
                same = jnp.logical_and(to_z == z, core == u)
                src = qm_ref.at[0, pl.ds(0, half), :]
                sent(src, s_q.at[d, u, 0], same)

                @pl.when(lax.rem(to_z, 2) == lax.rem(z, 2))
                def _():
                    sent(src, s_q.at[d, u, 1], same)


def main_head(z):
    return 3 * (z // 2) + 2 * lax.rem(z, 2)


def self_kernel(use_max, half, count, sc_half, kv_ref, qm_ref, qs_ref, sk_ref, out_ref, scene_ref,
                kv, qbuf, acc, best, ctx, s_z, s_s, s_q, s_yp, s_ym, s_co, s_sy, s_sc, s_c,
                r_kv, r_co, r_s, r_sy, r_sc, r_q, r_c):
    y, z, core = place()
    other = 1 - core
    block = NY * 2 * half
    up, down = lax.rem(y + 1, NY), lax.rem(y + NY - 1, NY)
    far = lax.rem(y + 2, NY)
    greet(y, z, core, True)
    send_queries(y, z, core, half, qm_ref, qs_ref, qbuf, s_q, r_q)

    def part(slot, of_y, u):
        return kv.at[pl.ds(slot * block + of_y * 2 * half + u * half, half), :]

    def each_target(body):
        for d in (4, 0, 1, 7, 2, 6, 3, 5):
            to_z = lax.rem(z + NZ - d, NZ)

            @pl.when(to_z // 4 == core)
            def _():
                for u in range(2):
                    same = jnp.logical_and(to_z == z, core == u)
                    body(d, to_z - 4 * core, u, device(y, to_z, u), same)

    def send_kv(d, j, u, to, same):
        c = [i for i in range(4) if d in ORDER[i]][0]
        slot = 2 * c + ORDER[c].index(d)
        put(None, kv_ref.at[j, pl.ds(u * half, half), :], part(slot, y, u), s_z.at[d, u], r_kv.at[y, slot], to, same)

    def scene_part(u, of_y):
        return scene_ref.at[pl.ds((u * NY + of_y) * NZ * sc_half, NZ * sc_half), :]

    def send_scene(d, j, u, to, same):
        dst = scene_ref.at[pl.ds((u * NY + y) * NZ * sc_half + z * sc_half, sc_half), :]
        put(None, sk_ref.at[j, pl.ds(u * sc_half, sc_half), :], dst, s_s.at[d, u], r_s.at[z], to, same)

    each_target(send_kv)
    each_target(send_scene)

    def share(of_y, slot):
        ref = part(slot, of_y, core)
        pltpu.make_async_remote_copy(
            ref, ref, s_co.at[of_y, slot], r_co.at[of_y, slot], device(y, z, other), MESH
        ).start()

    def pass_on(of_y, slot, to_y, sem):
        ref = part(slot, of_y, core)
        pltpu.make_async_remote_copy(ref, ref, sem, r_kv.at[of_y, slot], device(to_y, z, core), MESH).start()

    def own(c):
        for slot in (2 * c, 2 * c + 1):
            landed(part(slot, y, core), r_kv.at[y, slot])
            pass_on(y, slot, up, s_yp.at[0, slot])
            pass_on(y, slot, down, s_ym.at[0, slot])
            share(y, slot)

    def near(c):
        for s in range(2):
            slot = 2 * c + s
            landed(part(slot, down, core), r_kv.at[down, slot])
            if s == 0:
                pass_on(down, slot, up, s_yp.at[1, slot])
            share(down, slot)
            landed(part(slot, up, core), r_kv.at[up, slot])
            if s == 1:
                pass_on(up, slot, down, s_ym.at[1, slot])
            share(up, slot)

    def farther(c):
        for slot in (2 * c, 2 * c + 1):
            landed(part(slot, far, core), r_kv.at[far, slot])
            share(far, slot)

    def together(c):
        for of_y in range(NY):
            for slot in (2 * c, 2 * c + 1):
                landed(part(slot, of_y, other), r_co.at[of_y, slot])

    def compute(c, first):
        size = 2 * block
        keys = pl.ds(c * size, size)

        def main(i, unused):
            rows = pl.ds(i * count, count)
            attend(use_max, qbuf[rows, :], kv[keys, 0:128], kv[keys, 256:384], acc, best, rows)
            return unused

        def shared(i, unused):
            rows = pl.ds(i * count, count)
            attend(use_max, qbuf[rows, :], kv[keys, 128:256], kv[keys, 384:512], acc, best, rows)
            return unused

        n_main, n_all = NZ * half // count, (NZ + 4) * half // count
        if first:
            lax.fori_loop(0, n_main, main, 0)
        else:
            lax.fori_loop(n_main, n_all, shared, 0)

    acc[...] = jnp.zeros_like(acc)
    if use_max:
        best[...] = jnp.full_like(best, -1e30)
    own(0)
    near(0)
    farther(0)
    for i in range(12):
        landed(qbuf.at[pl.ds(i * half, half), :], r_q.at[i])
    for c in range(4):
        if c < 3:
            own(c + 1)
        together(c)
        compute(c, True)
        if c < 3:
            near(c + 1)
        compute(c, False)
        if c < 3:
            farther(c + 1)
        if c == 2:
            for i in range(NZ):
                landed(scene_ref.at[pl.ds(0, sc_half), :], r_s.at[i])
            for d in range(1, NY):
                ref = scene_part(core, y)
                pltpu.make_async_remote_copy(
                    ref, ref, s_sy.at[d - 1], r_sy.at[y], device(lax.rem(y + d, NY), z, core), MESH
                ).start()
    for i in range(12):
        rows = pl.ds(i * half, half)
        ctx[rows, :] = (acc[rows, 0:128] / acc[rows, 128:256]).astype(BF16)

    def each_context(body):
        for i in range(12):
            if i < NZ:
                to_z, head = lax.rem(z + i, NZ), main_head(z)
                row = to_z * half
            else:
                to_z, head = lax.rem(z, 2) + 2 * (i - NZ), 3 * (z // 2) + 1
                row = i * half
            same = to_z == z
            body(i, row, to_z, head, same)

    def send_context(i, row, to_z, head, same):
        cols = pl.ds(pl.multiple_of(head * HD, HD), HD)
        put(None, ctx.at[pl.ds(pl.multiple_of(row, 16), half), :], out_ref.at[:, cols], s_c.at[i], r_c.at[head],
            device(y, to_z, core), same)

    each_context(send_context)
    scene_size = scene_ref.at[pl.ds(0, NZ * sc_half), :]

    def share_scene(of_y):
        ref = scene_part(core, of_y)
        pltpu.make_async_remote_copy(
            ref, ref, s_sc.at[of_y], r_sc.at[of_y], device(y, z, other), MESH
        ).start()

    share_scene(y)
    for d in range(1, NY):
        of_y = lax.rem(y + d, NY)
        landed(scene_part(core, of_y), r_sy.at[of_y])
        share_scene(of_y)
    for of_y in range(NY):
        landed(scene_part(other, of_y), r_sc.at[of_y])
    for head in range(12):
        landed(out_ref.at[:, head * HD : (head + 1) * HD], r_c.at[head])
    queries_sent(y, z, core, half, qm_ref, qs_ref, s_q)
    packet = kv_ref.at[0, pl.ds(0, half), :]
    small = sk_ref.at[0, pl.ds(0, sc_half), :]
    each_target(lambda d, j, u, to, same: sent(packet, s_z.at[d, u], same))
    each_target(lambda d, j, u, to, same: sent(small, s_s.at[d, u], same))
    each_context(
        lambda i, row, to_z, head, same: sent(ctx.at[pl.ds(0, half), :], s_c.at[i], same)
    )
    for slot in range(8):
        landed(packet, s_yp.at[0, slot])
        landed(packet, s_ym.at[0, slot])
        landed(packet, s_yp.at[1, slot] if slot % 2 == 0 else s_ym.at[1, slot])
        for of_y in range(NY):
            landed(packet, s_co.at[of_y, slot])
    for i in range(NY):
        landed(scene_size, s_sc.at[i])
        if i < 3:
            landed(scene_size, s_sy.at[i])


def self_attention(use_max, packets, qm, qs, scene):
    half, sc_half = packets.shape[1] // 2, scene.shape[1] // 2
    dma = pltpu.SemaphoreType.DMA
    vmem = pl.BlockSpec(memory_space=pltpu.VMEM)
    body = functools.partial(self_kernel, use_max, half, 4 * half, sc_half)
    return pl.pallas_call(
        body,
        out_shape=(
            jax.ShapeDtypeStruct((half, 12 * HD), BF16),
            jax.ShapeDtypeStruct((2 * sc_half * NY * NZ, 4 * HD), BF16),
        ),
        in_specs=[vmem] * 4,
        out_specs=(vmem, vmem),
        scratch_shapes=[
            pltpu.VMEM((NY * NZ * 2 * half, 4 * HD), BF16),
            pltpu.VMEM((12 * half, HD), BF16),
            pltpu.VMEM((12 * half, 2 * HD), F32),
            pltpu.VMEM((12 * half, HD), F32),
            pltpu.VMEM((12 * half, HD), BF16),
            dma((8, 2)), dma((8, 2)), dma((8, 2, 2)), dma((2, 8)), dma((2, 8)), dma((4, 8)), dma((3,)), dma((4,)), dma((12,)),
            dma((4, 8)), dma((4, 8)), dma((8,)), dma((4,)), dma((4,)), dma((12,)), dma((12,)),
        ],
        compiler_params=pltpu.CompilerParams(
            collective_id=1 if use_max else 0, has_side_effects=True, vmem_limit_bytes=60 * 2**20
        ),
    )(packets, qm, qs, scene)


def cross_kernel(half, count, qm_ref, qs_ref, scene_ref, out_ref, qbuf, ctx, s_q, s_c, r_q, r_c):
    y, z, core = place()
    greet(y, z, core, False)
    send_queries(y, z, core, half, qm_ref, qs_ref, qbuf, s_q, r_q)
    for i in range(12):
        landed(qbuf.at[pl.ds(i * half, half), :], r_q.at[i])
    n_main, n_all = NZ * half // count, (NZ + 4) * half // count

    def one(at, i, unused):
        rows = pl.ds(i * count, count)
        keys, values = scene_ref[:, at * HD : at * HD + HD], scene_ref[:, (at + 2) * HD : (at + 3) * HD]
        s = lax.dot_general(
            qbuf[rows, :], keys, (((1,), (1,)), ((), ())), preferred_element_type=F32
        )
        best = jnp.max(s, axis=1, keepdims=True)
        p = jnp.exp2((s - best) * SCALE2).astype(BF16)
        wide = jnp.concatenate([values, jnp.ones_like(values)], axis=1)
        total = jnp.dot(p, wide, preferred_element_type=F32)
        ctx[rows, :] = (total[:, 0:128] / total[:, 128:256]).astype(BF16)
        return unused

    lax.fori_loop(0, n_main, functools.partial(one, 0), 0)
    lax.fori_loop(n_main, n_all, functools.partial(one, 1), 0)

    def each_context(body):
        for i in range(12):
            if i < NZ:
                to_z, head = lax.rem(z + i, NZ), main_head(z)
                row = to_z * half
            else:
                to_z, head = lax.rem(z, 2) + 2 * (i - NZ), 3 * (z // 2) + 1
                row = i * half
            same = jnp.logical_and(to_z == z, z // 4 == core)
            body(i, row, to_z, head - 6 * (z // 4), same)

    def send_context(i, row, to_z, head, same):
        cols = pl.ds(pl.multiple_of(head * HD, HD), HD)
        rows = pl.ds(pl.multiple_of(core * half, 16), half)
        put(None, ctx.at[pl.ds(pl.multiple_of(row, 16), half), :], out_ref.at[rows, cols], s_c.at[i],
            r_c.at[head, core], device(y, to_z, z // 4), same)

    each_context(send_context)
    for head in range(6):
        for u in range(2):
            landed(out_ref.at[pl.ds(u * half, half), head * HD : (head + 1) * HD], r_c.at[head, u])
    queries_sent(y, z, core, half, qm_ref, qs_ref, s_q)
    each_context(
        lambda i, row, to_z, head, same: sent(ctx.at[pl.ds(0, half), :], s_c.at[i], same)
    )


def cross_attention(qm, qs, scene):
    half = qm.shape[1] // 2
    dma = pltpu.SemaphoreType.DMA
    vmem = pl.BlockSpec(memory_space=pltpu.VMEM)
    return pl.pallas_call(
        functools.partial(cross_kernel, half, 4 * half),
        out_shape=jax.ShapeDtypeStruct((2 * half, 6 * HD), BF16),
        in_specs=[vmem] * 3,
        out_specs=vmem,
        scratch_shapes=[
            pltpu.VMEM((12 * half, HD), BF16),
            pltpu.VMEM((12 * half, HD), BF16),
            dma((8, 2, 2)), dma((12,)), dma((12,)), dma((6, 2)),
        ],
        compiler_params=pltpu.CompilerParams(
            collective_id=2, has_side_effects=True, vmem_limit_bytes=60 * 2**20
        ),
    )(qm, qs, scene)


def by_target(heads, which):
    return jnp.stack([heads[:, i] for i in which])


def shards(
    tokens, modulation, w_qkv, w_out, w_cross, q_gain, k_gain, cross_gain, scene_keys, scene_values
):
    width = tokens.shape[1]
    local_width = w_qkv.shape[2]
    heads_here = local_width // HD
    rows_raw = lax.all_gather(tokens, "head", axis=0, tiled=True)
    w_out_all = lax.all_gather(w_out, "head", axis=0, tiled=True)
    rows_count = rows_raw.shape[0]
    xfloat = rows_raw.astype(F32)
    mean = jnp.mean(xfloat, axis=-1, keepdims=True)
    var = jnp.mean((xfloat - mean) ** 2, axis=-1, keepdims=True)
    normed = (xfloat - mean) * lax.rsqrt(var + 1e-06)
    modulated = (normed * (1.0 + modulation[1]) + modulation[0]).astype(BF16)
    projected = jnp.dot(
        modulated, w_qkv.reshape(width, 3 * local_width), preferred_element_type=F32
    )
    projected = projected.reshape(rows_count, 3, heads_here, HD)
    queries = head_norm(projected[:, 0], q_gain).astype(BF16)
    keys = head_norm(projected[:, 1], k_gain).astype(BF16)
    values = projected[:, 2].astype(BF16)
    sides = (by_target(keys, MAIN), by_target(keys, SHARED), by_target(values, MAIN), by_target(values, SHARED))
    packets = jnp.concatenate(sides, axis=2)
    sk = scene_keys.reshape(-1, heads_here, HD)
    sv = scene_values.reshape(-1, heads_here, HD)
    scene = jnp.concatenate(
        (by_target(sk, MAIN), by_target(sk, SHARED), by_target(sv, MAIN), by_target(sv, SHARED)), axis=2
    )
    top = 1.02 * HD * SCALE2 * jnp.max(jnp.abs(q_gain)) * jnp.max(jnp.abs(k_gain))
    context, scene_all = lax.cond(
        top < SAFE_EXPONENT,
        functools.partial(self_attention, False),
        functools.partial(self_attention, True),
        packets, by_target(queries, MAIN), by_target(queries, SHARED), scene,
    )
    mine = jnp.dot(context, w_out_all, preferred_element_type=F32)
    hidden = (tokens.astype(F32) + modulation[2] * mine).astype(BF16)
    hidden_all = lax.all_gather(hidden, "head", axis=0, tiled=True)
    cross_proj = jnp.dot(hidden_all, w_cross, preferred_element_type=F32)
    cross_proj = cross_proj.reshape(rows_count, heads_here, HD)
    cross_queries = head_norm(cross_proj, cross_gain).astype(BF16)
    cross_context = cross_attention(by_target(cross_queries, MAIN), by_target(cross_queries, SHARED), scene_all)
    return (hidden, cross_context)


def solution(mesh):
    return jax.shard_map(
        shards,
        mesh=mesh,
        in_specs=(
            P(("clip", "blk", "head"), None),
            P("clip", None),
            P(None, None, "head"),
            P("head", None),
            P(None, "head"),
            P(),
            P(),
            P(),
            P(("clip", "blk"), "head"),
            P(("clip", "blk"), "head"),
        ),
        out_specs=(P(("clip", "blk", "head"), None), P(("clip", "blk"), "head")),
        check_vma=False,
    )
```

```python
import functools

import jax
import jax.numpy as jnp
from jax import lax
from jax.experimental import pallas as pl
from jax.experimental.pallas import tpu as pltpu
from jax.sharding import PartitionSpec as P

HD = 128
NY, NZ = 4, 8
F32, BF16 = jnp.float32, jnp.bfloat16
MESH = pl.DeviceIdType.MESH
SCALE2 = 1.4426950408889634 / HD**0.5
SAFE_EXPONENT = 96.0
MAIN = (0, 2, 3, 5)
SHARED = (1, 1, 4, 4)
ORDER = ((1, 7), (0, 4), (2, 6), (3, 5))


def head_norm(values, gain):
    rms = jnp.mean(values * values, axis=-1, keepdims=True)
    return values * lax.rsqrt(rms + 1e-06) * gain


def device(y, z, core):
    return {"blk": y * NZ + z, "head": core}


def source_core(z):
    return lax.rem(z // 2, 2)


def main_of(z):
    return 3 * (z // 4) + 2 * lax.rem(z, 2)


def shared_of(z):
    return 3 * (z // 4) + 1


def put(src, dst, send_sem, recv_sem, target, same):
    @pl.when(same)
    def _():
        pltpu.make_async_copy(src, dst, recv_sem).start()

    @pl.when(jnp.logical_not(same))
    def _():
        pltpu.make_async_remote_copy(src, dst, send_sem, recv_sem, target, MESH).start()


def landed(dst, recv_sem):
    pltpu.make_async_copy(dst, dst, recv_sem).wait()


def sent(src, send_sem, same):
    @pl.when(jnp.logical_not(same))
    def _():
        landed(src, send_sem)


def greet(y, z, core):
    barrier = pltpu.get_barrier_semaphore()
    for d in range(NZ):
        for e in range(2):
            if d or e:
                to = device(y, lax.rem(z + d, NZ), lax.rem(core + e, 2))
                pl.semaphore_signal(barrier, inc=1, device_id=to, device_id_type=MESH)
    for d in range(1, NY):
        to = device(lax.rem(y + d, NY), z, core)
        pl.semaphore_signal(barrier, inc=1, device_id=to, device_id_type=MESH)
    pl.semaphore_wait(barrier, 2 * NZ - 1 + NY - 1)


def scores_of(q, k):
    return lax.dot_general(q, k, (((1,), (1,)), ((), ())), preferred_element_type=F32)


def attend(use_max, q, k, v, acc, best, rows):
    s = scores_of(q, k)
    wide = jnp.concatenate([v, jnp.ones_like(v)], axis=1)
    if use_max:
        s = s * SCALE2
        old = best[rows, :]
        new = jnp.maximum(old, jnp.max(s, axis=1, keepdims=True))
        best[rows, :] = new
        p = jnp.exp2(s - new[:, :1]).astype(BF16)
        factor = jnp.exp2(old - new)
        kept = acc[rows, :] * jnp.concatenate([factor, factor], axis=1)
        acc[rows, :] = kept + jnp.dot(p, wide, preferred_element_type=F32)
    else:
        p = jnp.exp2(s * SCALE2).astype(BF16)
        acc[rows, :] += jnp.dot(p, wide, preferred_element_type=F32)


def block_kernel(
    use_max, half, sc_half,
    tok_ref, mod_ref, w_ref, wo_ref, wc_ref, qg_ref, kg_ref, cg_ref, sk_ref, sv_ref,
    hid_ref, out_ref,
    w, wo, wc, mod, kv_out, qm, qs, sc_out, kv, qbuf, acc, best, ctx, ctx_in, scene, hid, cqm, cqs, cqbuf,
    s_w, s_x, r_x, s_z, s_s, s_q, s_cq, s_yp, s_ym, s_co, s_sy, s_sc, s_c, s_cc,
    r_kv, r_co, r_s, r_sy, r_sc, r_q, r_cq, r_c, r_cc,
):
    blk = lax.axis_index("blk")
    y, z, core = blk // NZ, lax.rem(blk, NZ), lax.axis_index("head")
    other = 1 - core
    block = NY * 2 * half
    count = 4 * half
    deep = wo_ref.shape[0]
    up, down, far = lax.rem(y + 1, NY), lax.rem(y + NY - 1, NY), lax.rem(y + 2, NY)
    mine = pl.ds(pl.multiple_of(core * half, 16), half)
    theirs = pl.ds(pl.multiple_of(other * half, 16), half)
    my_rows = pl.ds(pl.multiple_of(core * deep, 16), deep)
    their_rows = pl.ds(pl.multiple_of(other * deep, 16), deep)

    for at, p in enumerate((1, 2, 0)):
        pltpu.make_async_copy(w_ref.at[p], w.at[p], s_w.at[p]).start()
    pltpu.make_async_copy(wo_ref, wo.at[my_rows, :], s_w.at[3]).start()
    pltpu.make_async_copy(wc_ref, wc, s_w.at[4]).start()
    x = tok_ref[...].astype(F32)
    mean = jnp.mean(x, axis=-1, keepdims=True)
    var = jnp.mean((x - mean) ** 2, axis=-1, keepdims=True)
    normed = (x - mean) * lax.rsqrt(var + 1e-06)
    mod[mine, :] = (normed * (1.0 + mod_ref[1:2, :]) + mod_ref[0:1, :]).astype(BF16)
    greet(y, z, core)
    sibling = device(y, z, other)

    def to_sibling(src, dst, i):
        return pltpu.make_async_remote_copy(src, dst, s_x.at[i], r_x.at[i], sibling, MESH)

    to_sibling(mod.at[mine, :], mod.at[mine, :], 0).start()
    landed(mod.at[theirs, :], r_x.at[0])
    to_sibling(wo_ref, wo.at[my_rows, :], 1).start()

    def project(left, weights, i):
        return jnp.dot(left[...], weights[:, 256 * i : 256 * i + 256], preferred_element_type=F32)

    for i in range(3):
        for at, h in ((0, 2 * i), (128, 2 * i + 1)):
            cols = slice(h * HD, (h + 1) * HD)
            for j in range(4):
                if MAIN[j] == h:
                    sc_out[j, :, 0:128] = sk_ref[:, cols]
                    sc_out[j, :, 256:384] = sv_ref[:, cols]
                if SHARED[j] == h:
                    sc_out[j, :, 128:256] = sk_ref[:, cols]
                    sc_out[j, :, 384:512] = sv_ref[:, cols]
    for p in (1, 2):
        landed(w.at[p], s_w.at[p])
        for i in range(3):
            whole = project(mod, w.at[p], i)
            for at, h in ((0, 2 * i), (128, 2 * i + 1)):
                part = whole[:, at : at + 128]
                part = (head_norm(part, kg_ref[...]) if p == 1 else part).astype(BF16)
                for j in range(4):
                    if MAIN[j] == h:
                        kv_out[j, :, (p - 1) * 256 : (p - 1) * 256 + 128] = part
                    if SHARED[j] == h:
                        kv_out[j, :, (p - 1) * 256 + 128 : (p - 1) * 256 + 256] = part

    def kv_part(slot, of_y, u):
        start = slot * block + of_y * 2 * half + u * half
        return kv.at[pl.ds(pl.multiple_of(start, 16), half), :]

    def each_target(order, body):
        for d in order:
            to_z = lax.rem(z + NZ - d, NZ)

            @pl.when(source_core(to_z) == core)
            def _():
                for u in range(2):
                    same = jnp.logical_and(to_z == z, core == u)
                    body(d, to_z, 2 * (to_z // 4) + lax.rem(to_z, 2), u, device(y, to_z, u), same)

    def send_kv(c):
        def one(d, to_z, j, u, to, same):
            slot = 2 * c + ORDER[c].index(d)
            put(kv_out.at[j, pl.ds(u * half, half), :], kv_part(slot, y, u), s_z.at[d, u], r_kv.at[y, slot], to, same)

        each_target(ORDER[c], one)

    def kv_sent(c):
        packet = kv_out.at[0, pl.ds(0, half), :]
        each_target(ORDER[c], lambda d, to_z, j, u, to, same: sent(packet, s_z.at[d, u], same))

    every = (4, 0, 1, 7, 2, 6, 3, 5)

    def send_queries(main, shared, into, s_sem, r_sem):
        def one(d, to_z, j, u, to, same):
            rows = pl.ds(u * half, half)
            there = pl.ds(pl.multiple_of(z * half, 16), half)
            put(main.at[j, rows, :], into.at[there, :], s_sem.at[d, u, 0], r_sem.at[z], to, same)

            @pl.when(lax.rem(to_z, 2) == lax.rem(z, 2))
            def _():
                unit = NZ + z // 2
                there = pl.ds(pl.multiple_of(unit * half, 16), half)
                put(shared.at[j, rows, :], into.at[there, :], s_sem.at[d, u, 1], r_sem.at[unit], to, same)

        each_target(every, one)

    def queries_sent(s_sem):
        src = qm.at[0, pl.ds(0, half), :]

        def one(d, to_z, j, u, to, same):
            sent(src, s_sem.at[d, u, 0], same)

            @pl.when(lax.rem(to_z, 2) == lax.rem(z, 2))
            def _():
                sent(src, s_sem.at[d, u, 1], same)

        each_target(every, one)

    def send_scene(d, to_z, j, u, to, same):
        start = (u * NY + y) * NZ * sc_half + z * sc_half
        dst = scene.at[pl.ds(pl.multiple_of(start, 16), sc_half), :]
        put(sc_out.at[j, pl.ds(u * sc_half, sc_half), :], dst, s_s.at[d, u], r_s.at[z], to, same)

    def share(of_y, slot):
        ref = kv_part(slot, of_y, core)
        pltpu.make_async_remote_copy(ref, ref, s_co.at[of_y, slot], r_co.at[of_y, slot], sibling, MESH).start()

    def pass_on(of_y, slot, to_y, sem):
        ref = kv_part(slot, of_y, core)
        pltpu.make_async_remote_copy(ref, ref, sem, r_kv.at[of_y, slot], device(to_y, z, core), MESH).start()

    def own(c):
        for s in range(2):
            slot = 2 * c + s
            landed(kv_part(slot, y, core), r_kv.at[y, slot])
            pass_on(y, slot, up, s_yp.at[0, slot])
            pass_on(y, slot, down, s_ym.at[0, slot])
            share(y, slot)

    def near(c):
        for s in range(2):
            slot = 2 * c + s
            landed(kv_part(slot, down, core), r_kv.at[down, slot])
            if s == 0:
                pass_on(down, slot, up, s_yp.at[1, slot])
            share(down, slot)
            landed(kv_part(slot, up, core), r_kv.at[up, slot])
            if s == 1:
                pass_on(up, slot, down, s_ym.at[1, slot])
            share(up, slot)

    def farther(c):
        for s in range(2):
            slot = 2 * c + s
            landed(kv_part(slot, far, core), r_kv.at[far, slot])
            share(far, slot)

    def together(c):
        for of_y in range(NY):
            for s in range(2):
                landed(kv_part(2 * c + s, of_y, other), r_co.at[of_y, 2 * c + s])

    def scene_part(u, of_y):
        start = (u * NY + of_y) * NZ * sc_half
        return scene.at[pl.ds(pl.multiple_of(start, 16), NZ * sc_half), :]

    def share_scene(of_y):
        ref = scene_part(core, of_y)
        pltpu.make_async_remote_copy(ref, ref, s_sc.at[of_y], r_sc.at[of_y], sibling, MESH).start()

    send_kv(0)
    send_kv(1)
    landed(w.at[0], s_w.at[0])
    for i in range(3):
        whole = project(mod, w.at[0], i)
        for at, h in ((0, 2 * i), (128, 2 * i + 1)):
            part = head_norm(whole[:, at : at + 128], qg_ref[...]).astype(BF16)
            for j in range(4):
                if MAIN[j] == h:
                    qm[j, :, :] = part
                if SHARED[j] == h:
                    qs[j, :, :] = part
    acc[...] = jnp.zeros_like(acc)
    if use_max:
        best[...] = jnp.full_like(best, -1e30)
    kv_sent(0)
    send_queries(qm, qs, qbuf, s_q, r_q)
    own(0)
    kv_sent(1)
    send_kv(2)
    own(1)
    near(0)
    queries_sent(s_q)
    send_kv(3)
    each_target(every, send_scene)
    farther(0)
    for i in range(12):
        landed(qbuf.at[pl.ds(i * half, half), :], r_q.at[i])

    def step(t, unused):
        c, i = t // 3, lax.rem(t, 3)

        @pl.when(i == 0)
        def _():
            together(c)

        rows = pl.ds(pl.multiple_of(i * count, 16), count)
        keys = pl.ds(pl.multiple_of(c * 2 * block, 16), 2 * block)
        at = (i // 2) * HD
        k_cols = pl.ds(pl.multiple_of(at, HD), HD)
        v_cols = pl.ds(pl.multiple_of(at + 2 * HD, HD), HD)
        attend(use_max, qbuf[rows, :], kv[keys, k_cols], kv[keys, v_cols], acc, best, rows)

        @pl.when(jnp.logical_and(i == 0, c < 3))
        def _():
            near(c + 1)

        @pl.when(jnp.logical_and(i == 1, c < 2))
        def _():
            own(c + 2)

        @pl.when(jnp.logical_and(i == 2, c < 3))
        def _():
            farther(c + 1)

        @pl.when(t == 7)
        def _():
            for k in range(NZ):
                landed(scene.at[pl.ds(0, sc_half), :], r_s.at[k])
            ref = scene_part(core, y)
            for d in range(1, NY):
                to = device(lax.rem(y + d, NY), z, core)
                pltpu.make_async_remote_copy(ref, ref, s_sy.at[d - 1], r_sy.at[y], to, MESH).start()
            share_scene(y)

        return unused

    lax.fori_loop(0, 12, step, 0)

    def each_context(body):
        for i in range(12):
            if i < NZ:
                to_z, head = lax.rem(z + i, NZ), main_of(z)
                row = to_z * half
            else:
                to_z, head = lax.rem(z, 2) + 2 * (i - NZ), shared_of(z)
                row = i * half
            body(i, ctx.at[pl.ds(pl.multiple_of(row, 16), half), :], to_z, head)

    def send_context(i, src, to_z, head):
        head = 6 * source_core(z) + head
        cols = pl.ds(pl.multiple_of(head * HD, HD), HD)
        put(src, ctx_in.at[:, cols], s_c.at[i], r_c.at[head], device(y, to_z, core), to_z == z)

    def send_cross(i, src, to_z, head):
        cols = pl.ds(pl.multiple_of(head * HD, HD), HD)
        to_core = source_core(z)
        same = jnp.logical_and(to_z == z, to_core == core)
        put(src, out_ref.at[mine, cols], s_cc.at[i], r_cc.at[head, core], device(y, to_z, to_core), same)

    for i in range(3):
        rows = pl.ds(i * count, count)
        ctx[rows, :] = (acc[rows, 0:128] / acc[rows, 128:256]).astype(BF16)
    each_context(send_context)
    for d in range(1, NY):
        of_y = lax.rem(y + d, NY)
        landed(scene_part(core, of_y), r_sy.at[of_y])
        share_scene(of_y)
    landed(wo.at[my_rows, :], s_w.at[3])
    landed(wc, s_w.at[4])
    landed(wo.at[their_rows, :], r_x.at[1])
    for head in range(12):
        landed(ctx_in.at[:, head * HD : (head + 1) * HD], r_c.at[head])
    for i in range(wo.shape[1] // 256):
        cols = slice(256 * i, 256 * i + 256)
        new = tok_ref[:, cols].astype(F32) + mod_ref[2:3, cols] * project(ctx_in, wo, i)
        hid_ref[:, cols] = new.astype(BF16)
        hid[mine, cols] = new.astype(BF16)
    to_sibling(hid.at[mine, :], hid.at[mine, :], 2).start()
    landed(hid.at[theirs, :], r_x.at[2])
    for i in range(3):
        whole = project(hid, wc, i)
        for at, h in ((0, 2 * i), (128, 2 * i + 1)):
            part = head_norm(whole[:, at : at + 128], cg_ref[...]).astype(BF16)
            for j in range(4):
                if MAIN[j] == h:
                    cqm[j, :, :] = part
                if SHARED[j] == h:
                    cqs[j, :, :] = part
    send_queries(cqm, cqs, cqbuf, s_cq, r_cq)
    small = sc_out.at[0, pl.ds(0, sc_half), :]
    kv_sent(2)
    kv_sent(3)
    each_target(every, lambda d, to_z, j, u, to, same: sent(small, s_s.at[d, u], same))
    each_context(lambda i, src, to_z, head: sent(ctx.at[pl.ds(0, half), :], s_c.at[i], to_z == z))
    packet = kv_out.at[0, pl.ds(0, half), :]
    for slot in range(8):
        landed(packet, s_yp.at[0, slot])
        landed(packet, s_ym.at[0, slot])
        landed(packet, s_yp.at[1, slot] if slot % 2 == 0 else s_ym.at[1, slot])
        for of_y in range(NY):
            landed(packet, s_co.at[of_y, slot])
    for i in range(NY):
        landed(scene_part(other, i), r_sc.at[i])
        landed(scene_part(0, 0), s_sc.at[i])
        if i < 3:
            landed(scene_part(0, 0), s_sy.at[i])
    landed(mod.at[mine, :], s_x.at[0])
    landed(wo_ref, s_x.at[1])
    landed(hid.at[mine, :], s_x.at[2])
    for i in range(12):
        landed(cqbuf.at[pl.ds(i * half, half), :], r_cq.at[i])

    def cross_step(i, unused):
        rows = pl.ds(pl.multiple_of(i * count, 16), count)
        at = (i // 2) * HD
        k_cols = pl.ds(pl.multiple_of(at, HD), HD)
        v_cols = pl.ds(pl.multiple_of(at + 2 * HD, HD), HD)
        s = scores_of(cqbuf[rows, :], scene[:, k_cols])
        p = jnp.exp2((s - jnp.max(s, axis=1, keepdims=True)) * SCALE2).astype(BF16)
        values = scene[:, v_cols]
        wide = jnp.concatenate([values, jnp.ones_like(values)], axis=1)
        total = jnp.dot(p, wide, preferred_element_type=F32)
        ctx[rows, :] = (total[:, 0:128] / total[:, 128:256]).astype(BF16)
        return unused

    lax.fori_loop(0, 3, cross_step, 0)
    each_context(send_cross)
    for head in range(6):
        for u in range(2):
            landed(out_ref.at[pl.ds(u * half, half), head * HD : (head + 1) * HD], r_cc.at[head, u])
    queries_sent(s_cq)

    def cross_sent(i, src, to_z, head):
        same = jnp.logical_and(to_z == z, source_core(z) == core)
        sent(ctx.at[pl.ds(0, half), :], s_cc.at[i], same)

    each_context(cross_sent)


def whole_block(use_max, tokens, modulation, w_parts, w_out, w_cross, q_gain, k_gain, c_gain, sk, sv):
    half, width = tokens.shape
    sc_half = sk.shape[0] // 2
    dma = pltpu.SemaphoreType.DMA
    vmem, anywhere = pl.BlockSpec(memory_space=pltpu.VMEM), pl.BlockSpec(memory_space=pl.ANY)
    sizes = [
        (w_parts.shape, BF16), ((2 * w_out.shape[0], width), BF16), (w_cross.shape, BF16), ((2 * half, width), BF16),
        ((4, 2 * half, 4 * HD), BF16), ((4, 2 * half, HD), BF16), ((4, 2 * half, HD), BF16),
        ((4, 2 * sc_half, 4 * HD), BF16),
        ((NY * NZ * 2 * half, 4 * HD), BF16), ((12 * half, HD), BF16),
        ((12 * half, 2 * HD), F32), ((12 * half, HD), F32), ((12 * half, HD), BF16), ((half, width), BF16),
        ((2 * sc_half * NY * NZ, 4 * HD), BF16), ((2 * half, width), BF16),
        ((4, 2 * half, HD), BF16), ((4, 2 * half, HD), BF16), ((12 * half, HD), BF16),
    ]
    sems = [
        (5,), (3,), (3,), (8, 2), (8, 2), (8, 2, 2), (8, 2, 2), (2, 8), (2, 8), (4, 8), (3,), (4,), (12,), (12,),
        (4, 8), (4, 8), (8,), (4,), (4,), (12,), (12,), (12,), (6, 2),
    ]
    return pl.pallas_call(
        functools.partial(block_kernel, use_max, half, sc_half),
        out_shape=(
            jax.ShapeDtypeStruct((half, width), BF16),
            jax.ShapeDtypeStruct((2 * half, 6 * HD), BF16),
        ),
        in_specs=[vmem, vmem, anywhere, anywhere, anywhere, vmem, vmem, vmem, vmem, vmem],
        out_specs=(vmem, vmem),
        scratch_shapes=[pltpu.VMEM(s, t) for s, t in sizes] + [dma(s) for s in sems],
        compiler_params=pltpu.CompilerParams(
            collective_id=1 if use_max else 0, has_side_effects=True, vmem_limit_bytes=60 * 2**20
        ),
    )(tokens, modulation, w_parts, w_out, w_cross, q_gain, k_gain, c_gain, sk, sv)


def shards(
    tokens, modulation, w_qkv, w_out, w_cross, q_gain, k_gain, cross_gain, scene_keys, scene_values
):
    top = 1.02 * HD * SCALE2 * jnp.max(jnp.abs(q_gain)) * jnp.max(jnp.abs(k_gain))
    return lax.cond(
        top < SAFE_EXPONENT,
        functools.partial(whole_block, False),
        functools.partial(whole_block, True),
        tokens, modulation, jnp.transpose(w_qkv, (1, 0, 2)), w_out, w_cross,
        q_gain[None], k_gain[None], cross_gain[None], scene_keys, scene_values,
    )


def solution(mesh):
    return jax.shard_map(
        shards,
        mesh=mesh,
        in_specs=(
            P(("clip", "blk", "head"), None),
            P("clip", None),
            P(None, None, "head"),
            P("head", None),
            P(None, "head"),
            P(),
            P(),
            P(),
            P(("clip", "blk"), "head"),
            P(("clip", "blk"), "head"),
        ),
        out_specs=(P(("clip", "blk", "head"), None), P(("clip", "blk"), "head")),
        check_vma=False,
    )
```

```python
import functools

import jax
import jax.numpy as jnp
from jax import lax
from jax.experimental import pallas as pl
from jax.experimental.pallas import tpu as pltpu
from jax.sharding import PartitionSpec as P

HD = 128
NY, NZ = 4, 8
F32, BF16 = jnp.float32, jnp.bfloat16
MESH = pl.DeviceIdType.MESH
SCALE2 = 1.4426950408889634 / HD**0.5
SAFE_EXPONENT = 96.0
MAIN = (0, 2, 3, 5)
SHARED = (1, 1, 4, 4)
ORDER = ((1, 7), (0, 4), (2, 6), (3, 5))
NEAREST = (0, 4, 1, 7, 2, 6, 3, 5)


def head_norm(values, gain):
    rms = jnp.mean(values * values, axis=-1, keepdims=True)
    return values * lax.rsqrt(rms + 1e-06) * gain


def device(y, z, core):
    return {"blk": y * NZ + z, "head": core}


def source_core(z):
    return lax.rem(z // 2, 2)


def main_of(z):
    return 3 * (z // 4) + 2 * lax.rem(z, 2)


def shared_of(z):
    return 3 * (z // 4) + 1


def put(src, dst, send_sem, recv_sem, target, same):
    @pl.when(same)
    def _():
        pltpu.make_async_copy(src, dst, recv_sem).start()

    @pl.when(jnp.logical_not(same))
    def _():
        pltpu.make_async_remote_copy(src, dst, send_sem, recv_sem, target, MESH).start()


def landed(dst, recv_sem):
    pltpu.make_async_copy(dst, dst, recv_sem).wait()


def sent(src, send_sem, same):
    @pl.when(jnp.logical_not(same))
    def _():
        landed(src, send_sem)


def greet(y, z, core):
    barrier = pltpu.get_barrier_semaphore()
    for d in range(NZ):
        for e in range(2):
            if d or e:
                to = device(y, lax.rem(z + d, NZ), lax.rem(core + e, 2))
                pl.semaphore_signal(barrier, inc=1, device_id=to, device_id_type=MESH)
    for d in range(1, NY):
        to = device(lax.rem(y + d, NY), z, core)
        pl.semaphore_signal(barrier, inc=1, device_id=to, device_id_type=MESH)


def scores_of(q, k):
    return lax.dot_general(q, k, (((1,), (1,)), ((), ())), preferred_element_type=F32)


def attend(use_max, q, k, v, acc, best, rows):
    s = scores_of(q, k)
    wide = jnp.concatenate([v, jnp.ones_like(v)], axis=1)
    if use_max:
        s = s * SCALE2
        old = best[rows, :]
        new = jnp.maximum(old, jnp.max(s, axis=1, keepdims=True))
        best[rows, :] = new
        p = jnp.exp2(s - new[:, :1]).astype(BF16)
        factor = jnp.exp2(old - new)
        kept = acc[rows, :] * jnp.concatenate([factor, factor], axis=1)
        acc[rows, :] = kept + jnp.dot(p, wide, preferred_element_type=F32)
    else:
        p = jnp.exp2(s * SCALE2).astype(BF16)
        acc[rows, :] += jnp.dot(p, wide, preferred_element_type=F32)


def block_kernel(
    use_max, half, sc_half,
    tok_ref, mod_ref, w_ref, wo_ref, wc_ref, qg_ref, kg_ref, cg_ref, sk_ref, sv_ref,
    hid_ref, out_ref,
    w, wo, wc, mod, kv_out, qm, qs, sc_out, kv, qbuf, acc, best, ctx, ctx_in, scene, hid, cqm, cqs, cqbuf,
    s_w, s_x, r_x, s_z, s_s, s_q, s_cq, s_yp, s_ym, s_co, s_sy, s_sc, s_c, s_cc,
    r_kv, r_co, r_s, r_sy, r_sc, r_q, r_cq, r_c, r_cc,
):
    blk = lax.axis_index("blk")
    y, z, core = blk // NZ, lax.rem(blk, NZ), lax.axis_index("head")
    other = 1 - core
    block = NY * 2 * half
    count = 4 * half
    deep = wo_ref.shape[0]
    up, down, far = lax.rem(y + 1, NY), lax.rem(y + NY - 1, NY), lax.rem(y + 2, NY)
    mine = pl.ds(pl.multiple_of(core * half, 16), half)
    theirs = pl.ds(pl.multiple_of(other * half, 16), half)
    my_rows = pl.ds(pl.multiple_of(core * deep, 16), deep)
    their_rows = pl.ds(pl.multiple_of(other * deep, 16), deep)

    greet(y, z, core)
    for p in (1, 2, 0):
        pltpu.make_async_copy(w_ref.at[p], w.at[p], s_w.at[p]).start()
    pltpu.make_async_copy(wo_ref, wo.at[my_rows, :], s_w.at[3]).start()
    pltpu.make_async_copy(wc_ref, wc, s_w.at[4]).start()
    x = tok_ref[...].astype(F32)
    mean = jnp.mean(x, axis=-1, keepdims=True)
    var = jnp.mean((x - mean) ** 2, axis=-1, keepdims=True)
    normed = (x - mean) * lax.rsqrt(var + 1e-06)
    mod[mine, :] = (normed * (1.0 + mod_ref[1:2, :]) + mod_ref[0:1, :]).astype(BF16)
    pl.semaphore_wait(pltpu.get_barrier_semaphore(), 2 * NZ - 1 + NY - 1)
    sibling = device(y, z, other)

    def to_sibling(src, dst, i):
        return pltpu.make_async_remote_copy(src, dst, s_x.at[i], r_x.at[i], sibling, MESH)

    to_sibling(mod.at[mine, :], mod.at[mine, :], 0).start()
    landed(mod.at[theirs, :], r_x.at[0])
    to_sibling(wo_ref, wo.at[my_rows, :], 1).start()

    def project(left, weights, i):
        return jnp.dot(left[...], weights[:, 256 * i : 256 * i + 256], preferred_element_type=F32)

    for i in range(3):
        for at, h in ((0, 2 * i), (128, 2 * i + 1)):
            cols = slice(h * HD, (h + 1) * HD)
            for j in range(4):
                if MAIN[j] == h:
                    sc_out[j, :, 0:128] = sk_ref[:, cols]
                    sc_out[j, :, 256:384] = sv_ref[:, cols]
                if SHARED[j] == h:
                    sc_out[j, :, 128:256] = sk_ref[:, cols]
                    sc_out[j, :, 384:512] = sv_ref[:, cols]
    for p in (1, 2):
        landed(w.at[p], s_w.at[p])
        for i in range(3):
            whole = project(mod, w.at[p], i)
            for at, h in ((0, 2 * i), (128, 2 * i + 1)):
                part = whole[:, at : at + 128]
                part = (head_norm(part, kg_ref[...]) if p == 1 else part).astype(BF16)
                for j in range(4):
                    if MAIN[j] == h:
                        kv_out[j, :, (p - 1) * 256 : (p - 1) * 256 + 128] = part
                    if SHARED[j] == h:
                        kv_out[j, :, (p - 1) * 256 + 128 : (p - 1) * 256 + 256] = part

    def kv_part(slot, of_y, u):
        start = slot * block + of_y * 2 * half + u * half
        return kv.at[pl.ds(pl.multiple_of(start, 16), half), :]

    def each_target(order, body):
        for d in order:
            to_z = lax.rem(z + NZ - d, NZ)

            @pl.when(source_core(to_z) == core)
            def _():
                for u in range(2):
                    same = jnp.logical_and(to_z == z, core == u)
                    body(d, to_z, 2 * (to_z // 4) + lax.rem(to_z, 2), u, device(y, to_z, u), same)

    def send_kv(c):
        def one(d, to_z, j, u, to, same):
            slot = 2 * c + ORDER[c].index(d)
            put(kv_out.at[j, pl.ds(u * half, half), :], kv_part(slot, y, u), s_z.at[d, u], r_kv.at[y, slot], to, same)

        each_target(ORDER[c], one)

    def kv_sent(c):
        packet = kv_out.at[0, pl.ds(0, half), :]
        each_target(ORDER[c], lambda d, to_z, j, u, to, same: sent(packet, s_z.at[d, u], same))

    def send_queries(main, shared, into, s_sem, r_sem):
        def one(d, to_z, j, u, to, same):
            unit = NEAREST.index(d)
            there = pl.ds(unit * half, half)
            put(main.at[j, pl.ds(u * half, half), :], into.at[there, :], s_sem.at[d, u, 0], r_sem.at[unit], to, same)

        def one_shared(d, to_z, j, u, to, same):
            unit = NZ + z // 2
            there = pl.ds(pl.multiple_of(unit * half, 16), half)
            put(shared.at[j, pl.ds(u * half, half), :], into.at[there, :], s_sem.at[d, u, 1], r_sem.at[unit], to, same)

        each_target(NEAREST, one)
        each_target((0, 4, 2, 6), one_shared)

    def queries_sent(s_sem):
        src = qm.at[0, pl.ds(0, half), :]
        each_target(NEAREST, lambda d, to_z, j, u, to, same: sent(src, s_sem.at[d, u, 0], same))
        each_target((0, 4, 2, 6), lambda d, to_z, j, u, to, same: sent(src, s_sem.at[d, u, 1], same))

    def send_scene(d, to_z, j, u, to, same):
        start = (u * NY + y) * NZ * sc_half + z * sc_half
        dst = scene.at[pl.ds(pl.multiple_of(start, 16), sc_half), :]
        put(sc_out.at[j, pl.ds(u * sc_half, sc_half), :], dst, s_s.at[d, u], r_s.at[z], to, same)

    def share(of_y, slot):
        ref = kv_part(slot, of_y, core)
        pltpu.make_async_remote_copy(ref, ref, s_co.at[of_y, slot], r_co.at[of_y, slot], sibling, MESH).start()

    def pass_on(of_y, slot, to_y, sem):
        ref = kv_part(slot, of_y, core)
        pltpu.make_async_remote_copy(ref, ref, sem, r_kv.at[of_y, slot], device(to_y, z, core), MESH).start()

    def own(c):
        for s in range(2):
            slot = 2 * c + s
            landed(kv_part(slot, y, core), r_kv.at[y, slot])
            pass_on(y, slot, up, s_yp.at[0, slot])
            pass_on(y, slot, down, s_ym.at[0, slot])
            share(y, slot)

    def near(c):
        for s in range(2):
            slot = 2 * c + s
            landed(kv_part(slot, down, core), r_kv.at[down, slot])
            if s == 0:
                pass_on(down, slot, up, s_yp.at[1, slot])
            share(down, slot)
            landed(kv_part(slot, up, core), r_kv.at[up, slot])
            if s == 1:
                pass_on(up, slot, down, s_ym.at[1, slot])
            share(up, slot)

    def farther(c):
        for s in range(2):
            slot = 2 * c + s
            landed(kv_part(slot, far, core), r_kv.at[far, slot])
            share(far, slot)

    def together(c):
        for of_y in range(NY):
            for s in range(2):
                landed(kv_part(2 * c + s, of_y, other), r_co.at[of_y, 2 * c + s])

    def scene_part(u, of_y):
        start = (u * NY + of_y) * NZ * sc_half
        return scene.at[pl.ds(pl.multiple_of(start, 16), NZ * sc_half), :]

    def share_scene(of_y):
        ref = scene_part(core, of_y)
        pltpu.make_async_remote_copy(ref, ref, s_sc.at[of_y], r_sc.at[of_y], sibling, MESH).start()

    send_kv(0)
    send_kv(1)
    landed(w.at[0], s_w.at[0])
    for i in range(3):
        whole = project(mod, w.at[0], i)
        for at, h in ((0, 2 * i), (128, 2 * i + 1)):
            part = head_norm(whole[:, at : at + 128], qg_ref[...]).astype(BF16)
            for j in range(4):
                if MAIN[j] == h:
                    qm[j, :, :] = part
                if SHARED[j] == h:
                    qs[j, :, :] = part
    acc[...] = jnp.zeros_like(acc)
    if use_max:
        best[...] = jnp.full_like(best, -1e30)
    kv_sent(0)
    send_queries(qm, qs, qbuf, s_q, r_q)
    own(0)
    kv_sent(1)
    send_kv(2)
    own(1)
    near(0)
    queries_sent(s_q)
    send_kv(3)
    near(1)
    farther(0)
    for i in range(12):
        landed(qbuf.at[pl.ds(i * half, half), :], r_q.at[i])

    def each_context(blocks, body):
        for i in [4 * b + k for b in blocks for k in range(4)]:
            if i < NZ:
                to_z, head = lax.rem(z + NEAREST[i], NZ), main_of(z)
            else:
                to_z, head = lax.rem(z, 2) + 2 * (i - NZ), shared_of(z)
            body(i, ctx.at[pl.ds(i * half, half), :], to_z, head)

    def send_context(i, src, to_z, head):
        head = 6 * source_core(z) + head
        cols = pl.ds(pl.multiple_of(head * HD, HD), HD)
        put(src, ctx_in.at[:, cols], s_c.at[i], r_c.at[head], device(y, to_z, core), to_z == z)

    def send_cross(i, src, to_z, head):
        cols = pl.ds(pl.multiple_of(head * HD, HD), HD)
        to_core = source_core(z)
        same = jnp.logical_and(to_z == z, to_core == core)
        put(src, out_ref.at[mine, cols], s_cc.at[i], r_cc.at[head, core], device(y, to_z, to_core), same)

    def step(t, unused):
        c, i = t // 3, lax.rem(t, 3)

        @pl.when(i == 0)
        def _():
            together(c)

        rows = pl.ds(pl.multiple_of(i * count, 16), count)
        keys = pl.ds(pl.multiple_of(c * 2 * block, 16), 2 * block)
        at = (i // 2) * HD
        k_cols = pl.ds(pl.multiple_of(at, HD), HD)
        v_cols = pl.ds(pl.multiple_of(at + 2 * HD, HD), HD)
        attend(use_max, qbuf[rows, :], kv[keys, k_cols], kv[keys, v_cols], acc, best, rows)

        @pl.when(jnp.logical_and(i == 0, c < 2))
        def _():
            own(c + 2)

        @pl.when(jnp.logical_or(jnp.logical_and(i == 1, c < 2), t == 6))
        def _():
            farther(c + 1)

        @pl.when(jnp.logical_and(i == 2, c < 2))
        def _():
            near(c + 2)

        @pl.when(t == 3)
        def _():
            each_target(NEAREST, send_scene)

        @pl.when(t == 6)
        def _():
            for k in range(NZ):
                landed(scene.at[pl.ds(0, sc_half), :], r_s.at[k])
            ref = scene_part(core, y)
            for d in range(1, NY):
                to = device(lax.rem(y + d, NY), z, core)
                pltpu.make_async_remote_copy(ref, ref, s_sy.at[d - 1], r_sy.at[y], to, MESH).start()
            share_scene(y)

        for last in range(3):

            @pl.when(t == 9 + last)
            def _():
                done = pl.ds(last * count, count)
                ctx[done, :] = (acc[done, 0:128] / acc[done, 128:256]).astype(BF16)
                each_context((last,), send_context)

        return unused

    lax.fori_loop(0, 12, step, 0)
    for d in range(1, NY):
        of_y = lax.rem(y + d, NY)
        landed(scene_part(core, of_y), r_sy.at[of_y])
        share_scene(of_y)
    landed(wo.at[my_rows, :], s_w.at[3])
    landed(wc, s_w.at[4])
    landed(wo.at[their_rows, :], r_x.at[1])
    for head in range(12):
        landed(ctx_in.at[:, head * HD : (head + 1) * HD], r_c.at[head])
    for i in range(wo.shape[1] // 256):
        cols = slice(256 * i, 256 * i + 256)
        new = tok_ref[:, cols].astype(F32) + mod_ref[2:3, cols] * project(ctx_in, wo, i)
        hid_ref[:, cols] = new.astype(BF16)
        hid[mine, cols] = new.astype(BF16)
    to_sibling(hid.at[mine, :], hid.at[mine, :], 2).start()
    landed(hid.at[theirs, :], r_x.at[2])
    for i in range(3):
        whole = project(hid, wc, i)
        for at, h in ((0, 2 * i), (128, 2 * i + 1)):
            part = head_norm(whole[:, at : at + 128], cg_ref[...]).astype(BF16)
            for j in range(4):
                if MAIN[j] == h:
                    cqm[j, :, :] = part
                if SHARED[j] == h:
                    cqs[j, :, :] = part
    send_queries(cqm, cqs, cqbuf, s_cq, r_cq)
    small = sc_out.at[0, pl.ds(0, sc_half), :]
    kv_sent(2)
    kv_sent(3)
    each_target(NEAREST, lambda d, to_z, j, u, to, same: sent(small, s_s.at[d, u], same))
    each_context((0, 1, 2), lambda i, src, to_z, head: sent(ctx.at[pl.ds(0, half), :], s_c.at[i], to_z == z))
    packet = kv_out.at[0, pl.ds(0, half), :]
    for slot in range(8):
        landed(packet, s_yp.at[0, slot])
        landed(packet, s_ym.at[0, slot])
        landed(packet, s_yp.at[1, slot] if slot % 2 == 0 else s_ym.at[1, slot])
        for of_y in range(NY):
            landed(packet, s_co.at[of_y, slot])
    for i in range(NY):
        landed(scene_part(other, i), r_sc.at[i])
        landed(scene_part(0, 0), s_sc.at[i])
        if i < 3:
            landed(scene_part(0, 0), s_sy.at[i])
    landed(mod.at[mine, :], s_x.at[0])
    landed(wo_ref, s_x.at[1])
    landed(hid.at[mine, :], s_x.at[2])

    def cross_step(i, unused):
        for k in range(4):
            unit = 4 * i + k
            landed(cqbuf.at[pl.ds(pl.multiple_of(unit * half, 16), half), :], r_cq.at[unit])
        rows = pl.ds(pl.multiple_of(i * count, 16), count)
        at = (i // 2) * HD
        k_cols = pl.ds(pl.multiple_of(at, HD), HD)
        v_cols = pl.ds(pl.multiple_of(at + 2 * HD, HD), HD)
        s = scores_of(cqbuf[rows, :], scene[:, k_cols])
        p = jnp.exp2((s - jnp.max(s, axis=1, keepdims=True)) * SCALE2).astype(BF16)
        values = scene[:, v_cols]
        wide = jnp.concatenate([values, jnp.ones_like(values)], axis=1)
        total = jnp.dot(p, wide, preferred_element_type=F32)
        ctx[rows, :] = (total[:, 0:128] / total[:, 128:256]).astype(BF16)
        for last in range(3):

            @pl.when(i == last)
            def _():
                each_context((last,), send_cross)

        return unused

    lax.fori_loop(0, 3, cross_step, 0)
    for head in range(6):
        for u in range(2):
            landed(out_ref.at[pl.ds(u * half, half), head * HD : (head + 1) * HD], r_cc.at[head, u])
    queries_sent(s_cq)

    def cross_sent(i, src, to_z, head):
        same = jnp.logical_and(to_z == z, source_core(z) == core)
        sent(ctx.at[pl.ds(0, half), :], s_cc.at[i], same)

    each_context((0, 1, 2), cross_sent)


def whole_block(use_max, tokens, modulation, w_parts, w_out, w_cross, q_gain, k_gain, c_gain, sk, sv):
    half, width = tokens.shape
    sc_half = sk.shape[0] // 2
    dma = pltpu.SemaphoreType.DMA
    vmem, anywhere = pl.BlockSpec(memory_space=pltpu.VMEM), pl.BlockSpec(memory_space=pl.ANY)
    sizes = [
        (w_parts.shape, BF16), ((2 * w_out.shape[0], width), BF16), (w_cross.shape, BF16), ((2 * half, width), BF16),
        ((4, 2 * half, 4 * HD), BF16), ((4, 2 * half, HD), BF16), ((4, 2 * half, HD), BF16),
        ((4, 2 * sc_half, 4 * HD), BF16),
        ((NY * NZ * 2 * half, 4 * HD), BF16), ((12 * half, HD), BF16),
        ((12 * half, 2 * HD), F32), ((12 * half, HD), F32), ((12 * half, HD), BF16), ((half, width), BF16),
        ((2 * sc_half * NY * NZ, 4 * HD), BF16), ((2 * half, width), BF16),
        ((4, 2 * half, HD), BF16), ((4, 2 * half, HD), BF16), ((12 * half, HD), BF16),
    ]
    sems = [
        (5,), (3,), (3,), (8, 2), (8, 2), (8, 2, 2), (8, 2, 2), (2, 8), (2, 8), (4, 8), (3,), (4,), (12,), (12,),
        (4, 8), (4, 8), (8,), (4,), (4,), (12,), (12,), (12,), (6, 2),
    ]
    return pl.pallas_call(
        functools.partial(block_kernel, use_max, half, sc_half),
        out_shape=(
            jax.ShapeDtypeStruct((half, width), BF16),
            jax.ShapeDtypeStruct((2 * half, 6 * HD), BF16),
        ),
        in_specs=[vmem, vmem, anywhere, anywhere, anywhere, vmem, vmem, vmem, vmem, vmem],
        out_specs=(vmem, vmem),
        scratch_shapes=[pltpu.VMEM(s, t) for s, t in sizes] + [dma(s) for s in sems],
        compiler_params=pltpu.CompilerParams(
            collective_id=1 if use_max else 0, has_side_effects=True, vmem_limit_bytes=60 * 2**20
        ),
    )(tokens, modulation, w_parts, w_out, w_cross, q_gain, k_gain, c_gain, sk, sv)


def shards(
    tokens, modulation, w_qkv, w_out, w_cross, q_gain, k_gain, cross_gain, scene_keys, scene_values
):
    top = 1.02 * HD * SCALE2 * jnp.max(jnp.abs(q_gain)[:, None] * jnp.abs(k_gain)[None, :])
    return lax.cond(
        top < SAFE_EXPONENT,
        functools.partial(whole_block, False),
        functools.partial(whole_block, True),
        tokens, modulation, jnp.transpose(w_qkv, (1, 0, 2)), w_out, w_cross,
        q_gain[None], k_gain[None], cross_gain[None], scene_keys, scene_values,
    )


def solution(mesh):
    return jax.shard_map(
        shards,
        mesh=mesh,
        in_specs=(
            P(("clip", "blk", "head"), None),
            P("clip", None),
            P(None, None, "head"),
            P("head", None),
            P(None, "head"),
            P(),
            P(),
            P(),
            P(("clip", "blk"), "head"),
            P(("clip", "blk"), "head"),
        ),
        out_specs=(P(("clip", "blk", "head"), None), P(("clip", "blk"), "head")),
        check_vma=False,
    )
```

```python
import functools

import jax
import jax.numpy as jnp
from jax import lax
from jax.experimental import pallas as pl
from jax.experimental.pallas import tpu as pltpu
from jax.sharding import PartitionSpec as P

HD = 128
NY, NZ = 4, 8
F32, BF16 = jnp.float32, jnp.bfloat16
MESH = pl.DeviceIdType.MESH
SCALE2 = 1.4426950408889634 / HD**0.5
SAFE_EXPONENT = 96.0
MAIN = (0, 2, 3, 5)
SHARED = (1, 1, 4, 4)
ORDER = ((1, 7), (0, 4), (2, 6), (3, 5))
NEAREST = (0, 4, 1, 7, 2, 6, 3, 5)


def head_norm(values, gain):
    rms = jnp.mean(values * values, axis=-1, keepdims=True)
    return values * lax.rsqrt(rms + 1e-06) * gain


def device(y, z, core):
    return {"blk": y * NZ + z, "head": core}


def source_core(z):
    return lax.rem(z // 2, 2)


def main_of(z):
    return 3 * (z // 4) + 2 * lax.rem(z, 2)


def shared_of(z):
    return 3 * (z // 4) + 1


def put(src, dst, send_sem, recv_sem, target, same):
    @pl.when(same)
    def _():
        pltpu.make_async_copy(src, dst, recv_sem).start()

    @pl.when(jnp.logical_not(same))
    def _():
        pltpu.make_async_remote_copy(src, dst, send_sem, recv_sem, target, MESH).start()


def landed(dst, recv_sem):
    pltpu.make_async_copy(dst, dst, recv_sem).wait()


def sent(src, send_sem, same):
    @pl.when(jnp.logical_not(same))
    def _():
        landed(src, send_sem)


def greet(y, z, core):
    barrier = pltpu.get_barrier_semaphore()
    for d in range(NZ):
        for e in range(2):
            if d or e:
                to = device(y, lax.rem(z + d, NZ), lax.rem(core + e, 2))
                pl.semaphore_signal(barrier, inc=1, device_id=to, device_id_type=MESH)
    for d in range(1, NY):
        for e in range(2):
            to = device(lax.rem(y + d, NY), z, lax.rem(core + e, 2))
            pl.semaphore_signal(barrier, inc=1, device_id=to, device_id_type=MESH)


def scores_of(q, k):
    return lax.dot_general(q, k, (((1,), (1,)), ((), ())), preferred_element_type=F32)


def attend(use_max, q, k, v, acc, best, rows):
    s = scores_of(q, k)
    wide = jnp.concatenate([v, jnp.ones_like(v)], axis=1)
    if use_max:
        s = s * SCALE2
        old = best[rows, :]
        new = jnp.maximum(old, jnp.max(s, axis=1, keepdims=True))
        best[rows, :] = new
        p = jnp.exp2(s - new[:, :1]).astype(BF16)
        factor = jnp.exp2(old - new)
        kept = acc[rows, :] * jnp.concatenate([factor, factor], axis=1)
        acc[rows, :] = kept + jnp.dot(p, wide, preferred_element_type=F32)
    else:
        p = jnp.exp2(s * SCALE2).astype(BF16)
        acc[rows, :] += jnp.dot(p, wide, preferred_element_type=F32)


def block_kernel(
    use_max, half, sc_half,
    tok_ref, mod_ref, w_ref, wo_ref, wc_ref, qg_ref, kg_ref, cg_ref, sk_ref, sv_ref,
    hid_ref, out_ref,
    w, wo, wc, mod, kv_out, qm, qs, sc_out, kv, qbuf, acc, best, ctx, ctx_in, scene, hid, cq, cqbuf,
    s_w, s_x, r_x, s_z, s_s, s_q, s_cq, s_yp, s_ym, s_co, s_su, s_sd, s_sc, s_c, s_cc,
    r_kv, r_co, r_s, r_sz, r_sc, r_q, r_cq, r_c, r_cc,
):
    blk = lax.axis_index("blk")
    y, z, core = blk // NZ, lax.rem(blk, NZ), lax.axis_index("head")
    other = 1 - core
    block = NY * 2 * half
    count = 4 * half
    deep = wo_ref.shape[0]
    up, down, far = lax.rem(y + 1, NY), lax.rem(y + NY - 1, NY), lax.rem(y + 2, NY)
    mine = pl.ds(pl.multiple_of(core * half, 16), half)
    theirs = pl.ds(pl.multiple_of(other * half, 16), half)
    my_rows = pl.ds(pl.multiple_of(core * deep, 16), deep)
    their_rows = pl.ds(pl.multiple_of(other * deep, 16), deep)

    greet(y, z, core)
    for p in (1, 2, 0):
        pltpu.make_async_copy(w_ref.at[p], w.at[p], s_w.at[p]).start()
    pltpu.make_async_copy(wo_ref, wo.at[my_rows, :], s_w.at[3]).start()
    pltpu.make_async_copy(wc_ref, wc, s_w.at[4]).start()
    x = tok_ref[...].astype(F32)
    mean = jnp.mean(x, axis=-1, keepdims=True)
    var = jnp.mean((x - mean) ** 2, axis=-1, keepdims=True)
    normed = (x - mean) * lax.rsqrt(var + 1e-06)
    mod[mine, :] = (normed * (1.0 + mod_ref[1:2, :]) + mod_ref[0:1, :]).astype(BF16)
    pl.semaphore_wait(pltpu.get_barrier_semaphore(), 2 * NZ - 1 + 2 * (NY - 1))
    sibling = device(y, z, other)

    def to_sibling(src, dst, i):
        return pltpu.make_async_remote_copy(src, dst, s_x.at[i], r_x.at[i], sibling, MESH)

    to_sibling(mod.at[mine, :], mod.at[mine, :], 0).start()
    three = 3 * HD
    for g in range(2):
        sc_out[g, :, 0:three] = sk_ref[:, g * three : (g + 1) * three]
        sc_out[g, :, three : 2 * three] = sv_ref[:, g * three : (g + 1) * three]
    landed(mod.at[theirs, :], r_x.at[0])
    to_sibling(wo_ref, wo.at[my_rows, :], 1).start()

    def project(left, weights, i):
        return jnp.dot(left[...], weights[:, 256 * i : 256 * i + 256], preferred_element_type=F32)

    def each_ring(body):
        for g in range(2):
            for u in range(2):
                to_y = 2 * core + g
                body(g, u, device(to_y, z, u), jnp.logical_and(to_y == y, core == u))

    def scene_part(u, of_z):
        start = (u * NZ + of_z) * NY * sc_half
        return scene.at[pl.ds(pl.multiple_of(start, 16), NY * sc_half), :]

    def send_scene(g, u, to, same):
        start = ((u * NZ + z) * NY + y) * sc_half
        dst = scene.at[pl.ds(pl.multiple_of(start, 16), sc_half), :]
        put(sc_out.at[g, pl.ds(u * sc_half, sc_half), :], dst, s_s.at[g, u], r_s.at[y], to, same)

    def pass_scene(of_z, d, sem):
        ref = scene_part(core, of_z)
        to = device(y, lax.rem(z + NZ + d, NZ), core)
        pltpu.make_async_remote_copy(ref, ref, sem, r_sz.at[of_z], to, MESH).start()

    def share_scene(of_z):
        ref = scene_part(core, of_z)
        pltpu.make_async_remote_copy(ref, ref, s_sc.at[of_z], r_sc.at[of_z], sibling, MESH).start()

    def ring_scene(k):
        if k == 0:
            for i in range(NY):
                landed(scene.at[pl.ds(0, sc_half), :], r_s.at[i])
            pass_scene(z, 1, s_su.at[0])
            pass_scene(z, -1, s_sd.at[0])
            share_scene(z)
            return
        below, above = lax.rem(z + NZ - k, NZ), lax.rem(z + k, NZ)
        landed(scene_part(core, below), r_sz.at[below])
        if k < 4:
            pass_scene(below, 1, s_su.at[k])
        share_scene(below)
        if k < 4:
            landed(scene_part(core, above), r_sz.at[above])
            if k < 3:
                pass_scene(above, -1, s_sd.at[k])
            share_scene(above)

    each_ring(send_scene)
    for p in (1, 2):
        landed(w.at[p], s_w.at[p])
        for i in range(3):
            whole = project(mod, w.at[p], i)
            for at, h in ((0, 2 * i), (128, 2 * i + 1)):
                part = whole[:, at : at + 128]
                part = (head_norm(part, kg_ref[...]) if p == 1 else part).astype(BF16)
                for j in range(4):
                    if MAIN[j] == h:
                        kv_out[j, :, (p - 1) * 256 : (p - 1) * 256 + 128] = part
                    if SHARED[j] == h:
                        kv_out[j, :, (p - 1) * 256 + 128 : (p - 1) * 256 + 256] = part

    def kv_part(slot, of_y, u):
        start = slot * block + of_y * 2 * half + u * half
        return kv.at[pl.ds(pl.multiple_of(start, 16), half), :]

    def each_target(order, body):
        for d in order:
            to_z = lax.rem(z + NZ - d, NZ)

            @pl.when(source_core(to_z) == core)
            def _():
                for u in range(2):
                    same = jnp.logical_and(to_z == z, core == u)
                    body(d, to_z, 2 * (to_z // 4) + lax.rem(to_z, 2), u, device(y, to_z, u), same)

    def send_kv(c):
        def one(d, to_z, j, u, to, same):
            slot = 2 * c + ORDER[c].index(d)
            put(kv_out.at[j, pl.ds(u * half, half), :], kv_part(slot, y, u), s_z.at[d, u], r_kv.at[y, slot], to, same)

        each_target(ORDER[c], one)

    def kv_sent(c):
        packet = kv_out.at[0, pl.ds(0, half), :]
        each_target(ORDER[c], lambda d, to_z, j, u, to, same: sent(packet, s_z.at[d, u], same))

    def send_main(order, main, into, s_sem, r_sem):
        def one(d, to_z, j, u, to, same):
            unit = NEAREST.index(d)
            there = pl.ds(unit * half, half)
            put(main.at[j, pl.ds(u * half, half), :], into.at[there, :], s_sem.at[d, u, 0], r_sem.at[unit], to, same)

        each_target(order, one)

    def send_shared(shared, into, s_sem, r_sem):
        def one(d, to_z, j, u, to, same):
            unit = NZ + z // 2
            there = pl.ds(pl.multiple_of(unit * half, 16), half)
            put(shared.at[j, pl.ds(u * half, half), :], into.at[there, :], s_sem.at[d, u, 1], r_sem.at[unit], to, same)

        each_target((0, 4, 2, 6), one)

    def queries_sent(order, s_sem, which):
        src = qm.at[0, pl.ds(0, half), :]
        each_target(order, lambda d, to_z, j, u, to, same: sent(src, s_sem.at[d, u, which], same))

    def share(of_y, slot):
        ref = kv_part(slot, of_y, core)
        pltpu.make_async_remote_copy(ref, ref, s_co.at[of_y, slot], r_co.at[of_y, slot], sibling, MESH).start()

    def pass_on(of_y, slot, to_y, sem):
        ref = kv_part(slot, of_y, core)
        pltpu.make_async_remote_copy(ref, ref, sem, r_kv.at[of_y, slot], device(to_y, z, core), MESH).start()

    def own(c):
        for s in range(2):
            slot = 2 * c + s
            landed(kv_part(slot, y, core), r_kv.at[y, slot])
            pass_on(y, slot, up, s_yp.at[0, slot])
            pass_on(y, slot, down, s_ym.at[0, slot])
            share(y, slot)

    def near(c):
        for s in range(2):
            slot = 2 * c + s
            landed(kv_part(slot, down, core), r_kv.at[down, slot])
            if s == 0:
                pass_on(down, slot, up, s_yp.at[1, slot])
            share(down, slot)
            landed(kv_part(slot, up, core), r_kv.at[up, slot])
            if s == 1:
                pass_on(up, slot, down, s_ym.at[1, slot])
            share(up, slot)

    def farther(c):
        for s in range(2):
            slot = 2 * c + s
            landed(kv_part(slot, far, core), r_kv.at[far, slot])
            share(far, slot)

    def together(c):
        for of_y in range(NY):
            for s in range(2):
                landed(kv_part(2 * c + s, of_y, other), r_co.at[of_y, 2 * c + s])

    send_kv(0)
    send_kv(1)
    landed(w.at[0], s_w.at[0])
    for i in range(3):
        whole = project(mod, w.at[0], i)
        for at, h in ((0, 2 * i), (128, 2 * i + 1)):
            part = head_norm(whole[:, at : at + 128], qg_ref[...]).astype(BF16)
            for j in range(4):
                if MAIN[j] == h:
                    qm[j, :, :] = part
                if SHARED[j] == h:
                    qs[j, :, :] = part
    acc[...] = jnp.zeros_like(acc)
    if use_max:
        best[...] = jnp.full_like(best, -1e30)
    kv_sent(0)
    send_main(NEAREST, qm, qbuf, s_q, r_q)
    own(0)
    kv_sent(1)
    send_kv(2)
    own(1)
    near(0)
    queries_sent(NEAREST, s_q, 0)
    send_kv(3)
    near(1)
    farther(0)
    ring_scene(0)
    for i in range(NZ):
        landed(qbuf.at[pl.ds(i * half, half), :], r_q.at[i])

    def each_context(blocks, body):
        for i in [4 * b + k for b in blocks for k in range(4)]:
            if i < NZ:
                to_z, head = lax.rem(z + NEAREST[i], NZ), main_of(z)
            else:
                to_z, head = lax.rem(z, 2) + 2 * (i - NZ), shared_of(z)
            body(i, ctx.at[pl.ds(i * half, half), :], to_z, head)

    def send_context(i, src, to_z, head):
        head = 6 * source_core(z) + head
        cols = pl.ds(pl.multiple_of(head * HD, HD), HD)
        put(src, ctx_in.at[:, cols], s_c.at[i], r_c.at[head], device(y, to_z, core), to_z == z)

    def each_cross(i, body):
        for k in range(NY):
            to_y, to_core = lax.rem(y + k, NY), y // 2
            same = jnp.logical_and(to_y == y, to_core == core)
            src = ctx.at[pl.ds(pl.multiple_of((i * NY + to_y) * half, 16), half), :]
            body(src, s_cc.at[i * NY + k], device(to_y, z, to_core), same)

    def send_cross(i, src, sem, to, same):
        head = 3 * lax.rem(y, 2) + i
        cols = pl.ds(pl.multiple_of(head * HD, HD), HD)
        put(src, out_ref.at[mine, cols], sem, r_cc.at[head, core], to, same)

    def start_shared():
        own(2)
        kv_sent(2)
        send_shared(qs, qbuf, s_q, r_q)

    def shared_here():
        for i in range(NZ, NZ + 4):
            landed(qbuf.at[pl.ds(i * half, half), :], r_q.at[i])

    def part_of(f, c):
        return functools.partial(f, c)

    before = {0: part_of(together, 0), 2: part_of(together, 1), 4: shared_here, 6: part_of(together, 2), 9: part_of(together, 3)}
    after = {
        0: (start_shared,), 1: (part_of(farther, 1), part_of(ring_scene, 1)), 2: (part_of(near, 2),), 3: (part_of(own, 3),),
        4: (part_of(farther, 2),), 5: (part_of(near, 3), part_of(ring_scene, 2),), 6: (part_of(farther, 3),), 7: (part_of(ring_scene, 3),), 8: (part_of(ring_scene, 4),),
    }

    def step(t, unused):
        late, odd = t // 6, lax.rem(t // 4, 2)
        c = late * (t // 3) + (1 - late) * ((1 - odd) * (t // 2) + odd * (t - 4))
        i = late * lax.rem(t, 3) + (1 - late) * ((1 - odd) * lax.rem(t, 2) + odd * 2)
        for when, action in before.items():
            pl.when(t == when)(action)
        rows = pl.ds(pl.multiple_of(i * count, 16), count)
        keys = pl.ds(pl.multiple_of(c * 2 * block, 16), 2 * block)
        at = (i // 2) * HD
        k_cols = pl.ds(pl.multiple_of(at, HD), HD)
        v_cols = pl.ds(pl.multiple_of(at + 2 * HD, HD), HD)
        attend(use_max, qbuf[rows, :], kv[keys, k_cols], kv[keys, v_cols], acc, best, rows)
        for when, actions in after.items():

            @pl.when(t == when)
            def _():
                for action in actions:
                    action()

        for last in range(3):

            @pl.when(t == 9 + last)
            def _():
                done = pl.ds(last * count, count)
                ctx[done, :] = (acc[done, 0:128] / acc[done, 128:256]).astype(BF16)
                each_context((last,), send_context)

        return unused

    lax.fori_loop(0, 12, step, 0)
    landed(wo.at[my_rows, :], s_w.at[3])
    landed(wc, s_w.at[4])
    landed(wo.at[their_rows, :], r_x.at[1])
    for head in range(12):
        landed(ctx_in.at[:, head * HD : (head + 1) * HD], r_c.at[head])
    for i in range(wo.shape[1] // 256):
        cols = slice(256 * i, 256 * i + 256)
        new = tok_ref[:, cols].astype(F32) + mod_ref[2:3, cols] * project(ctx_in, wo, i)
        hid_ref[:, cols] = new.astype(BF16)
        hid[mine, cols] = new.astype(BF16)
    to_sibling(hid.at[mine, :], hid.at[mine, :], 2).start()
    landed(hid.at[theirs, :], r_x.at[2])
    for i in range(3):
        whole = project(hid, wc, i)
        for at, h in ((0, 2 * i), (128, 2 * i + 1)):
            part = head_norm(whole[:, at : at + 128], cg_ref[...]).astype(BF16)
            cq[h, :, :] = part

    def send_cross_queries(i, g, u, to, same):
        there = pl.ds(pl.multiple_of((i * NY + y) * half, 16), half)
        src = cq.at[3 * g + i, pl.ds(u * half, half), :]
        put(src, cqbuf.at[there, :], s_cq.at[i, g, u], r_cq.at[i, y], to, same)

    for i in range(3):
        each_ring(functools.partial(send_cross_queries, i))
    small = sc_out.at[0, pl.ds(0, sc_half), :]
    unit = cq.at[0, pl.ds(0, half), :]
    kv_sent(3)
    queries_sent((0, 4, 2, 6), s_q, 1)
    each_ring(lambda g, u, to, same: sent(small, s_s.at[g, u], same))
    each_context((0, 1, 2), lambda i, src, to_z, head: sent(ctx.at[pl.ds(0, half), :], s_c.at[i], to_z == z))
    packet = kv_out.at[0, pl.ds(0, half), :]
    for slot in range(8):
        landed(packet, s_yp.at[0, slot])
        landed(packet, s_ym.at[0, slot])
        landed(packet, s_yp.at[1, slot] if slot % 2 == 0 else s_ym.at[1, slot])
        for of_y in range(NY):
            landed(packet, s_co.at[of_y, slot])
    for i in range(NZ):
        landed(scene_part(other, i), r_sc.at[i])
        landed(scene_part(core, i), s_sc.at[i])
    for i in range(4):
        landed(scene_part(core, 0), s_su.at[i])
        if i < 3:
            landed(scene_part(core, 0), s_sd.at[i])
    landed(mod.at[mine, :], s_x.at[0])
    landed(wo_ref, s_x.at[1])
    landed(hid.at[mine, :], s_x.at[2])

    def cross_step(i, unused):
        for k in range(NY):
            there = pl.ds(pl.multiple_of((i * NY + k) * half, 16), half)
            landed(cqbuf.at[there, :], r_cq.at[i, k])
        rows = pl.ds(pl.multiple_of(i * count, 16), count)
        k_cols = pl.ds(pl.multiple_of(i * HD, HD), HD)
        v_cols = pl.ds(pl.multiple_of((i + 3) * HD, HD), HD)
        s = scores_of(cqbuf[rows, :], scene[:, k_cols])
        p = jnp.exp2((s - jnp.max(s, axis=1, keepdims=True)) * SCALE2).astype(BF16)
        values = scene[:, v_cols]
        wide = jnp.concatenate([values, jnp.ones_like(values)], axis=1)
        total = jnp.dot(p, wide, preferred_element_type=F32)
        ctx[rows, :] = (total[:, 0:128] / total[:, 128:256]).astype(BF16)
        for last in range(3):

            @pl.when(i == last)
            def _():
                each_cross(last, functools.partial(send_cross, last))

        return unused

    lax.fori_loop(0, 3, cross_step, 0)
    for head in range(6):
        for u in range(2):
            landed(out_ref.at[pl.ds(u * half, half), head * HD : (head + 1) * HD], r_cc.at[head, u])
    for i in range(3):
        each_ring(lambda g, u, to, same: sent(unit, s_cq.at[i, g, u], same))
        each_cross(i, lambda src, sem, to, same: sent(unit, sem, same))


def whole_block(use_max, tokens, modulation, w_parts, w_out, w_cross, q_gain, k_gain, c_gain, sk, sv):
    half, width = tokens.shape
    sc_half = sk.shape[0] // 2
    dma = pltpu.SemaphoreType.DMA
    vmem, anywhere = pl.BlockSpec(memory_space=pltpu.VMEM), pl.BlockSpec(memory_space=pl.ANY)
    sizes = [
        (w_parts.shape, BF16), ((2 * w_out.shape[0], width), BF16), (w_cross.shape, BF16), ((2 * half, width), BF16),
        ((4, 2 * half, 4 * HD), BF16), ((4, 2 * half, HD), BF16), ((4, 2 * half, HD), BF16),
        ((2, 2 * sc_half, 6 * HD), BF16),
        ((NY * NZ * 2 * half, 4 * HD), BF16), ((12 * half, HD), BF16),
        ((12 * half, 2 * HD), F32), ((12 * half, HD), F32), ((12 * half, HD), BF16), ((half, width), BF16),
        ((2 * sc_half * NY * NZ, 6 * HD), BF16), ((2 * half, width), BF16),
        ((6, 2 * half, HD), BF16), ((12 * half, HD), BF16),
    ]
    sems = [
        (5,), (3,), (3,), (8, 2), (2, 2), (8, 2, 2), (3, 2, 2), (2, 8), (2, 8), (4, 8), (4,), (3,), (8,), (12,), (12,),
        (4, 8), (4, 8), (4,), (8,), (8,), (12,), (3, 4), (12,), (6, 2),
    ]
    return pl.pallas_call(
        functools.partial(block_kernel, use_max, half, sc_half),
        out_shape=(
            jax.ShapeDtypeStruct((half, width), BF16),
            jax.ShapeDtypeStruct((2 * half, 6 * HD), BF16),
        ),
        in_specs=[vmem, vmem, anywhere, anywhere, anywhere, vmem, vmem, vmem, vmem, vmem],
        out_specs=(vmem, vmem),
        scratch_shapes=[pltpu.VMEM(s, t) for s, t in sizes] + [dma(s) for s in sems],
        compiler_params=pltpu.CompilerParams(
            collective_id=1 if use_max else 0, has_side_effects=True, vmem_limit_bytes=60 * 2**20
        ),
    )(tokens, modulation, w_parts, w_out, w_cross, q_gain, k_gain, c_gain, sk, sv)


def shards(
    tokens, modulation, w_qkv, w_out, w_cross, q_gain, k_gain, cross_gain, scene_keys, scene_values
):
    top = 1.02 * HD * SCALE2 * jnp.max(jnp.abs(q_gain)[:, None] * jnp.abs(k_gain)[None, :])
    return lax.cond(
        top < SAFE_EXPONENT,
        functools.partial(whole_block, False),
        functools.partial(whole_block, True),
        tokens, modulation, jnp.transpose(w_qkv, (1, 0, 2)), w_out, w_cross,
        q_gain[None], k_gain[None], cross_gain[None], scene_keys, scene_values,
    )


def solution(mesh):
    return jax.shard_map(
        shards,
        mesh=mesh,
        in_specs=(
            P(("clip", "blk", "head"), None),
            P("clip", None),
            P(None, None, "head"),
            P("head", None),
            P(None, "head"),
            P(),
            P(),
            P(),
            P(("clip", "blk"), "head"),
            P(("clip", "blk"), "head"),
        ),
        out_specs=(P(("clip", "blk", "head"), None), P(("clip", "blk"), "head")),
        check_vma=False,
    )
```

```python
import functools

import jax
import jax.numpy as jnp
from jax import lax
from jax.experimental import pallas as pl
from jax.experimental.pallas import tpu as pltpu
from jax.sharding import PartitionSpec as P

HD = 128
NY, NZ = 4, 8
F32, BF16 = jnp.float32, jnp.bfloat16
MESH = pl.DeviceIdType.MESH
SCALE2 = 1.4426950408889634 / HD**0.5
SAFE_EXPONENT = 96.0
MAIN = (0, 2, 3, 5)
SHARED = (1, 1, 4, 4)
ORDER = ((1, 7), (0, 4), (2, 6), (3, 5))
NEAREST = (0, 4, 1, 7, 2, 6, 3, 5)


def head_norm(values, gain):
    rms = jnp.mean(values * values, axis=-1, keepdims=True)
    return values * lax.rsqrt(rms + 1e-06) * gain


def device(y, z, core):
    return {"blk": y * NZ + z, "head": core}


def source_core(z):
    return lax.rem(z // 2, 2)


def main_of(z):
    return 3 * (z // 4) + 2 * lax.rem(z, 2)


def shared_of(z):
    return 3 * (z // 4) + 1


def put(src, dst, send_sem, recv_sem, target, same):
    @pl.when(same)
    def _():
        pltpu.make_async_copy(src, dst, recv_sem).start()

    @pl.when(jnp.logical_not(same))
    def _():
        pltpu.make_async_remote_copy(src, dst, send_sem, recv_sem, target, MESH).start()


def landed(dst, recv_sem):
    pltpu.make_async_copy(dst, dst, recv_sem).wait()


def sent(src, send_sem, same):
    @pl.when(jnp.logical_not(same))
    def _():
        landed(src, send_sem)


def greet(y, z, core):
    barrier = pltpu.get_barrier_semaphore()
    for d in range(NZ):
        for e in range(2):
            if d or e:
                to = device(y, lax.rem(z + d, NZ), lax.rem(core + e, 2))
                pl.semaphore_signal(barrier, inc=1, device_id=to, device_id_type=MESH)
    for d in range(1, NY):
        for e in range(2):
            to = device(lax.rem(y + d, NY), z, lax.rem(core + e, 2))
            pl.semaphore_signal(barrier, inc=1, device_id=to, device_id_type=MESH)


def scores_of(q, k):
    return lax.dot_general(q, k, (((1,), (1,)), ((), ())), preferred_element_type=F32)


def attend(use_max, q, k, v, acc, best, rows):
    s = scores_of(q, k)
    wide = jnp.concatenate([v, jnp.ones_like(v)], axis=1)
    if use_max:
        s = s * SCALE2
        old = best[rows, :]
        new = jnp.maximum(old, jnp.max(s, axis=1, keepdims=True))
        best[rows, :] = new
        p = jnp.exp2(s - new[:, :1]).astype(BF16)
        factor = jnp.exp2(old - new)
        kept = acc[rows, :] * jnp.concatenate([factor, factor], axis=1)
        acc[rows, :] = kept + jnp.dot(p, wide, preferred_element_type=F32)
    else:
        p = jnp.exp2(s * SCALE2).astype(BF16)
        acc[rows, :] += jnp.dot(p, wide, preferred_element_type=F32)


def block_kernel(
    use_max, half, sc_half,
    tok_ref, mod_ref, w_ref, wo_ref, wc_ref, qg_ref, kg_ref, cg_ref, sk_ref, sv_ref,
    hid_ref, out_ref,
    w, wo, wc, mod, kv_out, qm, qs, sc_out, kv, qbuf, acc, best, ctx, ctx_in, scene, hid, cq, cqbuf,
    s_w, s_x, r_x, s_z, s_s, s_q, s_cq, s_yp, s_ym, s_co, s_su, s_sd, s_sc, s_c, s_cc,
    r_kv, r_co, r_s, r_sz, r_sc, r_q, r_cq, r_c, r_cc,
):
    blk = lax.axis_index("blk")
    y, z, core = blk // NZ, lax.rem(blk, NZ), lax.axis_index("head")
    other = 1 - core
    block = NY * 2 * half
    count = 4 * half
    deep = wo_ref.shape[0]
    up, down, far = lax.rem(y + 1, NY), lax.rem(y + NY - 1, NY), lax.rem(y + 2, NY)
    mine = pl.ds(pl.multiple_of(core * half, 16), half)
    theirs = pl.ds(pl.multiple_of(other * half, 16), half)
    my_rows = pl.ds(pl.multiple_of(core * deep, 16), deep)
    their_rows = pl.ds(pl.multiple_of(other * deep, 16), deep)

    greet(y, z, core)
    for p in (1, 2, 0):
        pltpu.make_async_copy(w_ref.at[p], w.at[p], s_w.at[p]).start()
    pltpu.make_async_copy(wo_ref, wo.at[my_rows, :], s_w.at[3]).start()
    pltpu.make_async_copy(wc_ref, wc, s_w.at[4]).start()
    x = tok_ref[...].astype(F32)
    mean = jnp.mean(x, axis=-1, keepdims=True)
    var = jnp.mean((x - mean) ** 2, axis=-1, keepdims=True)
    normed = (x - mean) * lax.rsqrt(var + 1e-06)
    mod[mine, :] = (normed * (1.0 + mod_ref[1:2, :]) + mod_ref[0:1, :]).astype(BF16)
    pl.semaphore_wait(pltpu.get_barrier_semaphore(), 2 * NZ - 1 + 2 * (NY - 1))
    sibling = device(y, z, other)

    def to_sibling(src, dst, i):
        return pltpu.make_async_remote_copy(src, dst, s_x.at[i], r_x.at[i], sibling, MESH)

    to_sibling(mod.at[mine, :], mod.at[mine, :], 0).start()
    three = 3 * HD
    for g in range(2):
        sc_out[g, :, 0:three] = sk_ref[:, g * three : (g + 1) * three]
        sc_out[g, :, three : 2 * three] = sv_ref[:, g * three : (g + 1) * three]
    landed(mod.at[theirs, :], r_x.at[0])
    to_sibling(wo_ref, wo.at[my_rows, :], 1).start()

    def project(left, weights, i):
        return jnp.dot(left[...], weights[:, 256 * i : 256 * i + 256], preferred_element_type=F32)

    def each_ring(body):
        for g in range(2):
            for u in range(2):
                to_y = 2 * core + g
                body(g, u, device(to_y, z, u), jnp.logical_and(to_y == y, core == u))

    def scene_part(u, of_z):
        start = (u * NZ + of_z) * NY * sc_half
        return scene.at[pl.ds(pl.multiple_of(start, 16), NY * sc_half), :]

    def send_scene(g, u, to, same):
        start = ((u * NZ + z) * NY + y) * sc_half
        dst = scene.at[pl.ds(pl.multiple_of(start, 16), sc_half), :]
        put(sc_out.at[g, pl.ds(u * sc_half, sc_half), :], dst, s_s.at[g, u], r_s.at[y], to, same)

    def pass_scene(of_z, d, sem):
        ref = scene_part(core, of_z)
        to = device(y, lax.rem(z + NZ + d, NZ), core)
        pltpu.make_async_remote_copy(ref, ref, sem, r_sz.at[of_z], to, MESH).start()

    def share_scene(of_z):
        ref = scene_part(core, of_z)
        pltpu.make_async_remote_copy(ref, ref, s_sc.at[of_z], r_sc.at[of_z], sibling, MESH).start()

    def ring_scene(k):
        if k == 0:
            for i in range(NY):
                landed(scene.at[pl.ds(0, sc_half), :], r_s.at[i])
            pass_scene(z, 1, s_su.at[0])
            pass_scene(z, -1, s_sd.at[0])
            share_scene(z)
            return
        below, above = lax.rem(z + NZ - k, NZ), lax.rem(z + k, NZ)
        landed(scene_part(core, below), r_sz.at[below])
        if k < 4:
            pass_scene(below, 1, s_su.at[k])
        share_scene(below)
        if k < 4:
            landed(scene_part(core, above), r_sz.at[above])
            if k < 3:
                pass_scene(above, -1, s_sd.at[k])
            share_scene(above)

    each_ring(send_scene)
    for p in (1, 2):
        landed(w.at[p], s_w.at[p])
        for i in range(3):
            whole = project(mod, w.at[p], i)
            for at, h in ((0, 2 * i), (128, 2 * i + 1)):
                part = whole[:, at : at + 128]
                part = (head_norm(part, kg_ref[...]) if p == 1 else part).astype(BF16)
                for j in range(4):
                    if MAIN[j] == h:
                        kv_out[j, :, (p - 1) * 256 : (p - 1) * 256 + 128] = part
                    if SHARED[j] == h:
                        kv_out[j, :, (p - 1) * 256 + 128 : (p - 1) * 256 + 256] = part

    def kv_part(slot, of_y, u):
        start = slot * block + of_y * 2 * half + u * half
        return kv.at[pl.ds(pl.multiple_of(start, 16), half), :]

    def each_target(order, body):
        for d in order:
            to_z = lax.rem(z + NZ - d, NZ)

            @pl.when(source_core(to_z) == core)
            def _():
                for u in range(2):
                    same = jnp.logical_and(to_z == z, core == u)
                    body(d, to_z, 2 * (to_z // 4) + lax.rem(to_z, 2), u, device(y, to_z, u), same)

    def send_kv(c):
        def one(d, to_z, j, u, to, same):
            slot = 2 * c + ORDER[c].index(d)
            put(kv_out.at[j, pl.ds(u * half, half), :], kv_part(slot, y, u), s_z.at[d, u], r_kv.at[y, slot], to, same)

        each_target(ORDER[c], one)

    def kv_sent(c):
        packet = kv_out.at[0, pl.ds(0, half), :]
        each_target(ORDER[c], lambda d, to_z, j, u, to, same: sent(packet, s_z.at[d, u], same))

    def send_main(order, main, into, s_sem, r_sem):
        def one(d, to_z, j, u, to, same):
            unit = NEAREST.index(d)
            there = pl.ds(unit * half, half)
            put(main.at[j, pl.ds(u * half, half), :], into.at[there, :], s_sem.at[d, u, 0], r_sem.at[unit], to, same)

        each_target(order, one)

    def send_shared(shared, into, s_sem, r_sem):
        def one(d, to_z, j, u, to, same):
            unit = NZ + z // 2
            there = pl.ds(pl.multiple_of(unit * half, 16), half)
            put(shared.at[j, pl.ds(u * half, half), :], into.at[there, :], s_sem.at[d, u, 1], r_sem.at[unit], to, same)

        each_target((0, 4, 2, 6), one)

    def queries_sent(order, s_sem, which):
        src = qm.at[0, pl.ds(0, half), :]
        each_target(order, lambda d, to_z, j, u, to, same: sent(src, s_sem.at[d, u, which], same))

    def share(of_y, slot):
        ref = kv_part(slot, of_y, core)
        pltpu.make_async_remote_copy(ref, ref, s_co.at[of_y, slot], r_co.at[of_y, slot], sibling, MESH).start()

    def pass_on(of_y, slot, to_y, sem):
        ref = kv_part(slot, of_y, core)
        pltpu.make_async_remote_copy(ref, ref, sem, r_kv.at[of_y, slot], device(to_y, z, core), MESH).start()

    def own(c):
        for s in range(2):
            slot = 2 * c + s
            landed(kv_part(slot, y, core), r_kv.at[y, slot])
            pass_on(y, slot, up, s_yp.at[0, slot])
            pass_on(y, slot, down, s_ym.at[0, slot])
            share(y, slot)

    def near(c):
        for s in range(2):
            slot = 2 * c + s
            landed(kv_part(slot, down, core), r_kv.at[down, slot])
            if s == 0:
                pass_on(down, slot, up, s_yp.at[1, slot])
            share(down, slot)
            landed(kv_part(slot, up, core), r_kv.at[up, slot])
            if s == 1:
                pass_on(up, slot, down, s_ym.at[1, slot])
            share(up, slot)

    def farther(c):
        for s in range(2):
            slot = 2 * c + s
            landed(kv_part(slot, far, core), r_kv.at[far, slot])
            share(far, slot)

    def together(c):
        for of_y in range(NY):
            for s in range(2):
                landed(kv_part(2 * c + s, of_y, other), r_co.at[of_y, 2 * c + s])

    send_kv(0)
    send_kv(1)
    landed(w.at[0], s_w.at[0])
    for i in range(3):
        whole = project(mod, w.at[0], i)
        for at, h in ((0, 2 * i), (128, 2 * i + 1)):
            part = head_norm(whole[:, at : at + 128], qg_ref[...]).astype(BF16)
            for j in range(4):
                if MAIN[j] == h:
                    qm[j, :, :] = part
                if SHARED[j] == h:
                    qs[j, :, :] = part
    acc[...] = jnp.zeros_like(acc)
    if use_max:
        best[...] = jnp.full_like(best, -1e30)
    kv_sent(0)
    send_main(NEAREST, qm, qbuf, s_q, r_q)
    own(0)
    kv_sent(1)
    send_kv(2)
    own(1)
    near(0)
    queries_sent(NEAREST, s_q, 0)
    send_kv(3)
    near(1)
    farther(0)
    ring_scene(0)
    for i in range(NZ):
        landed(qbuf.at[pl.ds(i * half, half), :], r_q.at[i])

    def each_context(blocks, body):
        for i in [4 * b + k for b in blocks for k in range(4)]:
            if i < NZ:
                to_z, head = lax.rem(z + NEAREST[i], NZ), main_of(z)
            else:
                to_z, head = lax.rem(z, 2) + 2 * (i - NZ), shared_of(z)
            body(i, ctx.at[pl.ds(i * half, half), :], to_z, head)

    def send_context(i, src, to_z, head):
        head = 6 * source_core(z) + head
        cols = pl.ds(pl.multiple_of(head * HD, HD), HD)
        put(src, ctx_in.at[:, cols], s_c.at[i], r_c.at[head], device(y, to_z, core), to_z == z)

    def each_cross(i, body):
        for k in range(NY):
            to_y, to_core = lax.rem(y + k, NY), y // 2
            same = jnp.logical_and(to_y == y, to_core == core)
            src = ctx.at[pl.ds(pl.multiple_of((i * NY + to_y) * half, 16), half), :]
            body(src, s_cc.at[i * NY + k], device(to_y, z, to_core), same)

    def send_cross(i, src, sem, to, same):
        head = 3 * lax.rem(y, 2) + i
        cols = pl.ds(pl.multiple_of(head * HD, HD), HD)
        put(src, out_ref.at[mine, cols], sem, r_cc.at[head, core], to, same)

    def start_shared():
        own(2)
        kv_sent(2)
        send_shared(qs, qbuf, s_q, r_q)

    def shared_here():
        for i in range(NZ, NZ + 4):
            landed(qbuf.at[pl.ds(i * half, half), :], r_q.at[i])

    def part_of(f, c):
        return functools.partial(f, c)

    before = {0: part_of(together, 0), 2: part_of(together, 1), 4: shared_here, 6: part_of(together, 2), 9: part_of(together, 3)}
    after = {
        0: (start_shared,), 1: (part_of(farther, 1), part_of(ring_scene, 1)), 2: (part_of(near, 2),), 3: (part_of(own, 3),),
        4: (part_of(farther, 2),), 5: (part_of(near, 3), part_of(ring_scene, 2),), 6: (part_of(farther, 3),), 8: (part_of(ring_scene, 3),),
    }

    def step(t, unused):
        late, odd = t // 6, lax.rem(t // 4, 2)
        c = late * (t // 3) + (1 - late) * ((1 - odd) * (t // 2) + odd * (t - 4))
        i = late * lax.rem(t, 3) + (1 - late) * ((1 - odd) * lax.rem(t, 2) + odd * 2)
        for when, action in before.items():
            pl.when(t == when)(action)
        rows = pl.ds(pl.multiple_of(i * count, 16), count)
        keys = pl.ds(pl.multiple_of(c * 2 * block, 16), 2 * block)
        at = (i // 2) * HD
        k_cols = pl.ds(pl.multiple_of(at, HD), HD)
        v_cols = pl.ds(pl.multiple_of(at + 2 * HD, HD), HD)
        attend(use_max, qbuf[rows, :], kv[keys, k_cols], kv[keys, v_cols], acc, best, rows)
        for when, actions in after.items():

            @pl.when(t == when)
            def _():
                for action in actions:
                    action()

        for last in range(3):

            @pl.when(t == 9 + last)
            def _():
                done = pl.ds(last * count, count)
                ctx[done, :] = (acc[done, 0:128] / acc[done, 128:256]).astype(BF16)
                each_context((last,), send_context)

        return unused

    lax.fori_loop(0, 12, step, 0)
    ring_scene(4)
    landed(wo.at[my_rows, :], s_w.at[3])
    landed(wc, s_w.at[4])
    landed(wo.at[their_rows, :], r_x.at[1])
    for head in range(12):
        landed(ctx_in.at[:, head * HD : (head + 1) * HD], r_c.at[head])
    for i in range(wo.shape[1] // 256):
        cols = slice(256 * i, 256 * i + 256)
        new = tok_ref[:, cols].astype(F32) + mod_ref[2:3, cols] * project(ctx_in, wo, i)
        hid_ref[:, cols] = new.astype(BF16)
        hid[mine, cols] = new.astype(BF16)
    to_sibling(hid.at[mine, :], hid.at[mine, :], 2).start()
    landed(hid.at[theirs, :], r_x.at[2])
    for i in range(3):
        whole = project(hid, wc, i)
        for at, h in ((0, 2 * i), (128, 2 * i + 1)):
            part = head_norm(whole[:, at : at + 128], cg_ref[...]).astype(BF16)
            cq[h, :, :] = part

    def send_cross_queries(i, g, u, to, same):
        there = pl.ds(pl.multiple_of((i * NY + y) * half, 16), half)
        src = cq.at[3 * g + i, pl.ds(u * half, half), :]
        put(src, cqbuf.at[there, :], s_cq.at[i, g, u], r_cq.at[i, y], to, same)

    for i in range(3):
        each_ring(functools.partial(send_cross_queries, i))
    small = sc_out.at[0, pl.ds(0, sc_half), :]
    unit = cq.at[0, pl.ds(0, half), :]
    kv_sent(3)
    queries_sent((0, 4, 2, 6), s_q, 1)
    each_ring(lambda g, u, to, same: sent(small, s_s.at[g, u], same))
    each_context((0, 1, 2), lambda i, src, to_z, head: sent(ctx.at[pl.ds(0, half), :], s_c.at[i], to_z == z))
    packet = kv_out.at[0, pl.ds(0, half), :]
    for slot in range(8):
        landed(packet, s_yp.at[0, slot])
        landed(packet, s_ym.at[0, slot])
        landed(packet, s_yp.at[1, slot] if slot % 2 == 0 else s_ym.at[1, slot])
        for of_y in range(NY):
            landed(packet, s_co.at[of_y, slot])
    for i in range(NZ):
        landed(scene_part(other, i), r_sc.at[i])
        landed(scene_part(core, i), s_sc.at[i])
    for i in range(4):
        landed(scene_part(core, 0), s_su.at[i])
        if i < 3:
            landed(scene_part(core, 0), s_sd.at[i])
    landed(mod.at[mine, :], s_x.at[0])
    landed(wo_ref, s_x.at[1])
    landed(hid.at[mine, :], s_x.at[2])

    def cross_step(i, unused):
        for k in range(NY):
            there = pl.ds(pl.multiple_of((i * NY + k) * half, 16), half)
            landed(cqbuf.at[there, :], r_cq.at[i, k])
        rows = pl.ds(pl.multiple_of(i * count, 16), count)
        k_cols = pl.ds(pl.multiple_of(i * HD, HD), HD)
        v_cols = pl.ds(pl.multiple_of((i + 3) * HD, HD), HD)
        s = scores_of(cqbuf[rows, :], scene[:, k_cols])
        p = jnp.exp2((s - jnp.max(s, axis=1, keepdims=True)) * SCALE2).astype(BF16)
        values = scene[:, v_cols]
        wide = jnp.concatenate([values, jnp.ones_like(values)], axis=1)
        total = jnp.dot(p, wide, preferred_element_type=F32)
        ctx[rows, :] = (total[:, 0:128] / total[:, 128:256]).astype(BF16)
        for last in range(3):

            @pl.when(i == last)
            def _():
                each_cross(last, functools.partial(send_cross, last))

        return unused

    lax.fori_loop(0, 3, cross_step, 0)
    for head in range(6):
        for u in range(2):
            landed(out_ref.at[pl.ds(u * half, half), head * HD : (head + 1) * HD], r_cc.at[head, u])
    for i in range(3):
        each_ring(lambda g, u, to, same: sent(unit, s_cq.at[i, g, u], same))
        each_cross(i, lambda src, sem, to, same: sent(unit, sem, same))


def whole_block(use_max, tokens, modulation, w_parts, w_out, w_cross, q_gain, k_gain, c_gain, sk, sv):
    half, width = tokens.shape
    sc_half = sk.shape[0] // 2
    dma = pltpu.SemaphoreType.DMA
    vmem, anywhere = pl.BlockSpec(memory_space=pltpu.VMEM), pl.BlockSpec(memory_space=pl.ANY)
    sizes = [
        (w_parts.shape, BF16), ((2 * w_out.shape[0], width), BF16), (w_cross.shape, BF16), ((2 * half, width), BF16),
        ((4, 2 * half, 4 * HD), BF16), ((4, 2 * half, HD), BF16), ((4, 2 * half, HD), BF16),
        ((2, 2 * sc_half, 6 * HD), BF16),
        ((NY * NZ * 2 * half, 4 * HD), BF16), ((12 * half, HD), BF16),
        ((12 * half, 2 * HD), F32), ((12 * half, HD), F32), ((12 * half, HD), BF16), ((half, width), BF16),
        ((2 * sc_half * NY * NZ, 6 * HD), BF16), ((2 * half, width), BF16),
        ((6, 2 * half, HD), BF16), ((12 * half, HD), BF16),
    ]
    sems = [
        (5,), (3,), (3,), (8, 2), (2, 2), (8, 2, 2), (3, 2, 2), (2, 8), (2, 8), (4, 8), (4,), (3,), (8,), (12,), (12,),
        (4, 8), (4, 8), (4,), (8,), (8,), (12,), (3, 4), (12,), (6, 2),
    ]
    return pl.pallas_call(
        functools.partial(block_kernel, use_max, half, sc_half),
        out_shape=(
            jax.ShapeDtypeStruct((half, width), BF16),
            jax.ShapeDtypeStruct((2 * half, 6 * HD), BF16),
        ),
        in_specs=[vmem, vmem, anywhere, anywhere, anywhere, vmem, vmem, vmem, vmem, vmem],
        out_specs=(vmem, vmem),
        scratch_shapes=[pltpu.VMEM(s, t) for s, t in sizes] + [dma(s) for s in sems],
        compiler_params=pltpu.CompilerParams(
            collective_id=1 if use_max else 0, has_side_effects=True, vmem_limit_bytes=60 * 2**20
        ),
    )(tokens, modulation, w_parts, w_out, w_cross, q_gain, k_gain, c_gain, sk, sv)


def shards(
    tokens, modulation, w_qkv, w_out, w_cross, q_gain, k_gain, cross_gain, scene_keys, scene_values
):
    top = 1.02 * HD * SCALE2 * jnp.max(jnp.abs(q_gain)[:, None] * jnp.abs(k_gain)[None, :])
    return lax.cond(
        top < SAFE_EXPONENT,
        functools.partial(whole_block, False),
        functools.partial(whole_block, True),
        tokens, modulation, jnp.transpose(w_qkv, (1, 0, 2)), w_out, w_cross,
        q_gain[None], k_gain[None], cross_gain[None], scene_keys, scene_values,
    )


def solution(mesh):
    return jax.shard_map(
        shards,
        mesh=mesh,
        in_specs=(
            P(("clip", "blk", "head"), None),
            P("clip", None),
            P(None, None, "head"),
            P("head", None),
            P(None, "head"),
            P(),
            P(),
            P(),
            P(("clip", "blk"), "head"),
            P(("clip", "blk"), "head"),
        ),
        out_specs=(P(("clip", "blk", "head"), None), P(("clip", "blk"), "head")),
        check_vma=False,
    )
```
